256 devices in a mesh: seq: 64 (over x, y_lo, z), head: 2 (over core), dp: 2 (over y_hi).
Axes of the slice: x: 4, y: 4 (y_hi: 2, y_lo: 2; y = y_hi * 2 + y_lo), z: 8, core: 2. Of those that a mesh axis runs over, the one named last changes fastest.
Arguments:
- tokens: bfloat16 [24576, 1024], P(('dp', 'seq')), parts along dimension 0, may hold values from -6 to 6
- frame_order: int32 [128], P(('dp', 'seq')), parts along dimension 0, may hold values from 0 to 63, each once
- target_mask: int32 [128], P(('dp', 'seq')), parts along dimension 0, may hold values 0 or 1
- pose_norm: float32 [1024], replicated, may hold values from 0.25 to 1.75
- pose_qkv: bfloat16 [3, 1024, 1024], P(None, None, 'head'), may hold values from -0.1875 to 0.1875
- pose_out: bfloat16 [1024, 1024], P('head'), may hold values from -0.1875 to 0.1875
- camera_head: float32 [1024, 12], replicated, may hold values from -0.1875 to 0.1875
- ray_embed: float32 [6, 1024], replicated, may hold values from -2.5 to 2.5
- render_norm: float32 [1024], replicated, may hold values from 0.25 to 1.75
- render_qkv: bfloat16 [3, 1024, 1024], P(None, None, 'head'), as said below
- render_out: bfloat16 [1024, 1024], P('head'), may hold values from -0.1875 to 0.1875
Outputs:
- rendered: bfloat16 [24576, 1024], P(('dp', 'seq'), 'head'), parts along dimension 0
- cameras: float32 [128, 12], P(('dp', 'seq')), parts along dimension 0
The draws below stay inside these ranges and needn't reach their ends.
There are 2 independent parts, one for each index of `dp`. The reference program is written for one: setup_inputs(seed, part) draws one part's arguments, and reference() takes and returns one part's arrays. A program takes and returns all parts, laid end to end along the dimension named above; an argument that names none is the same for every part. Nothing has to cross between parts.
Inputs may be any that keep to these rules, and one draw needn't show every extreme that they name: `frame_order`: each frame's time index once. `render_qkv`: entries of magnitude at most 9 / sqrt(1024).
All inputs are finite; a program needn't handle non-finite values. No bound on the sum of `target_mask` on one device may be relied on, other than what follows from the above.
Results may differ from the reference program's by a relative error of at most 0.023.
Values may be sent and summed in bfloat16 or wider, within the bound.
No kernel may reach another device: no remote copies, remote signals or barrier semaphores. Data moves between devices by JAX's collectives and lax.ppermute only.
A program may use at most 128 MiB of HBM per device.

```python
import jax
import jax.numpy as jnp
from jax import lax

D = 1024
HEADS = 16
HEAD_DIM = 64
GRID = 32
CAM = 12
PATCH_DEV = 192
FRAMES = 64
TOKENS = 12288


def draw_render_qkv(key, part):
    key = jax.random.fold_in(key, 7)
    factors = jnp.array([1.5, 1.5, 1.0], jnp.float32)[:, None, None] * D ** (-0.5)
    base = jax.random.truncated_normal(key, -6.0, 6.0, (3, D, D), jnp.float32)
    return (base * factors).astype(jnp.bfloat16)


def with_ends(entries, key, least, high):
    shape = entries.shape
    spot = [jax.random.randint(jax.random.fold_in(key, axis), (), 0, shape[axis]) for axis in range(len(shape))]
    entries = entries.at[tuple(spot)].set(least)
    longest = shape.index(max(shape))
    spot[longest] = (spot[longest] + 1) % shape[longest]
    return entries.at[tuple(spot)].set(high)


def level_of(own_key, dims, split, smallest, high):
    level = 1.0
    for axis_at, parts in split:
        draws = jax.random.uniform(jax.random.fold_in(jax.random.fold_in(own_key, 6), axis_at), (parts,), jnp.float32, smallest / len(split), high / len(split))
        level = level * jnp.repeat(jnp.exp(draws), dims[axis_at] // parts).reshape((-1,) + (1,) * (len(dims) - 1 - axis_at))
    return level


def gaussian(rng, extent, spread, limit, pieces=(), kind=jnp.bfloat16):
    drawn = jax.random.normal(rng, extent, jnp.float32) * spread
    if len(pieces) > 0:
        drawn = level_of(rng, extent, pieces, -0.22, 0.18) * drawn
    return jnp.clip(drawn, min=-limit, max=limit).astype(kind)


def setup_inputs(seed: int = 0, part: int = 0) -> dict:
    key_list = jax.random.split(jax.random.key(seed), 12)
    own_keys = jax.random.split(jax.random.fold_in(key_list[11], part), 12)
    tokens = gaussian(own_keys[0], (TOKENS, D), 1.0, 6.0, ((0, 64),))
    frame_order = jax.random.permutation(own_keys[1], FRAMES).astype(jnp.int32)
    target_mask = with_ends((jax.random.randint(own_keys[2], (FRAMES,), 0, 4) < 1).astype(jnp.int32), jax.random.fold_in(own_keys[2], 1), 0, 1)
    pose_norm = jnp.clip(1.0 + 0.15 * jax.random.normal(key_list[3], (D,), jnp.float32), 0.25, 1.75)
    pose_qkv = gaussian(key_list[4], (3, D, D), D ** -0.5, 0.1875, ((2, 2),))
    pose_out = gaussian(key_list[5], (D, D), D ** -0.5, 0.1875, ((0, 2),))
    camera_head = gaussian(key_list[6], (D, CAM), D ** -0.5, 0.1875, (), jnp.float32)
    ray_embed = gaussian(key_list[7], (6, D), 6 ** -0.5, 2.5, (), jnp.float32)
    render_norm = jnp.clip(1.0 + 0.15 * jax.random.normal(key_list[8], (D,), jnp.float32), 0.25, 1.75)
    render_qkv = draw_render_qkv(jax.random.fold_in(key_list[11], 71), part)
    render_out = gaussian(key_list[10], (D, D), D ** -0.5, 0.1875, ((0, 2),))
    return {"tokens": tokens, "frame_order": frame_order, "target_mask": target_mask, "pose_norm": pose_norm, "pose_qkv": pose_qkv, "pose_out": pose_out, "camera_head": camera_head, "ray_embed": ray_embed, "render_norm": render_norm, "render_qkv": render_qkv, "render_out": render_out}


def rms_norm(values, gain):
    return values * lax.rsqrt(lax.optimization_barrier(jnp.mean(values * values, axis=-1, keepdims=True)) + 1e-06) * gain

def attend(query, keys, values):
    count = query.shape[0]
    query_h = query.astype(jnp.float32).reshape(count, HEADS, HEAD_DIM)
    keys_h = keys.astype(jnp.float32).reshape(keys.shape[0], HEADS, HEAD_DIM)
    values_h = values.astype(jnp.float32).reshape(values.shape[0], HEADS, HEAD_DIM)
    scores = jnp.einsum('qhd,khd->qhk', query_h, keys_h) * (1.0 / HEAD_DIM ** 0.5)
    top = lax.optimization_barrier(jnp.max(scores, axis=-1, keepdims=True))
    weights = jnp.exp(scores - top)
    total = lax.optimization_barrier(jnp.sum(weights, axis=-1))
    rounded = weights.astype(jnp.bfloat16).astype(jnp.float32)
    mixed = jnp.einsum('qhk,khd->qhd', rounded, values_h) / total[:, :, None]
    return mixed.reshape(count, D).astype(jnp.bfloat16)

def ray_features(cameras, count):
    index = jnp.arange(count, dtype=jnp.int32)
    across = ((index % GRID).astype(jnp.float32) + 0.5) * (2.0 / GRID) - 1.0
    down = ((index // GRID).astype(jnp.float32) + 0.5) * (2.0 / GRID) - 1.0
    turn = jnp.tanh(cameras[:, 0:9]) * 0.3
    place = jnp.tanh(cameras[:, 9:12]) * 2.0

    def entry(which):
        return turn[:, which][:, None]
    dir_one = (1.0 + entry(0)) * across + entry(1) * down + entry(2)
    dir_two = entry(3) * across + (1.0 + entry(4)) * down + entry(5)
    dir_three = entry(6) * across + entry(7) * down + (1.0 + entry(8))
    length = jnp.sqrt(dir_one * dir_one + dir_two * dir_two + dir_three * dir_three)
    unit_one, unit_two, unit_three = (dir_one / length, dir_two / length, dir_three / length)
    place_one, place_two, place_three = (place[:, 0][:, None], place[:, 1][:, None], place[:, 2][:, None])
    moment_one = place_two * unit_three - place_three * unit_two
    moment_two = place_three * unit_one - place_one * unit_three
    moment_three = place_one * unit_two - place_two * unit_one
    return jnp.stack([unit_one, unit_two, unit_three, moment_one, moment_two, moment_three], axis=0)

def reference(tokens, frame_order, target_mask, pose_norm, pose_qkv, pose_out, camera_head, ray_embed, render_norm, render_qkv, render_out):
    frame_rows = tokens.astype(jnp.float32).reshape(FRAMES, PATCH_DEV, D)
    pooled = lax.optimization_barrier(jnp.mean(frame_rows, axis=1))
    rate = jnp.exp(-4.0 * jnp.arange(D, dtype=jnp.float32) / D)
    cam_in = (pooled + jnp.sin(frame_order.astype(jnp.float32)[:, None] * rate[None, :])).astype(jnp.bfloat16)
    pose_in = rms_norm(cam_in.astype(jnp.float32), pose_norm).astype(jnp.bfloat16)
    pose_q = jnp.dot(pose_in, pose_qkv[0], preferred_element_type=jnp.float32).astype(jnp.bfloat16)
    pose_k = jnp.dot(pose_in, pose_qkv[1], preferred_element_type=jnp.float32).astype(jnp.bfloat16)
    pose_v = jnp.dot(pose_in, pose_qkv[2], preferred_element_type=jnp.float32).astype(jnp.bfloat16)
    pose_att = attend(pose_q, pose_k, pose_v)
    camera_tok = cam_in.astype(jnp.float32) + jnp.dot(pose_att, pose_out, preferred_element_type=jnp.float32)
    cameras = jnp.dot(camera_tok, camera_head, precision=lax.Precision.HIGHEST)
    rays = ray_features(cameras, PATCH_DEV)
    embedded = jnp.einsum('cfp,cd->fpd', rays, ray_embed, precision=lax.Precision.HIGHEST)
    keep = (1 - target_mask).astype(jnp.float32)[:, None, None]
    inputs = (keep * frame_rows + embedded).astype(jnp.bfloat16).reshape(TOKENS, D)
    render_in = rms_norm(inputs.astype(jnp.float32), render_norm).astype(jnp.bfloat16)
    render_q = jnp.dot(render_in, render_qkv[0], preferred_element_type=jnp.float32).astype(jnp.bfloat16)
    render_k = jnp.dot(render_in, render_qkv[1], preferred_element_type=jnp.float32).astype(jnp.bfloat16)
    render_v = jnp.dot(render_in, render_qkv[2], preferred_element_type=jnp.float32).astype(jnp.bfloat16)
    query_blocks = render_q.reshape(FRAMES, PATCH_DEV, D)
    attended = lax.map(lambda block: attend(block, render_k, render_v), query_blocks).reshape(TOKENS, D)
    rendered = inputs.astype(jnp.float32) + jnp.dot(attended, render_out, preferred_element_type=jnp.float32)
    return (rendered.astype(jnp.bfloat16), cameras)
```

```python
import jax
import jax.numpy as jnp
from jax import lax
from jax.experimental import pallas as pl
from jax.experimental.pallas import tpu as pltpu
from jax.sharding import Mesh
from jax.sharding import PartitionSpec as P

F32 = jnp.float32
BF16 = jnp.bfloat16
HEAD_DIM = 64
GRID = 32
ROWS = 192
WIDTH = 1024
HALF = 512
HEADS = 8
PAIRS = 4
GROUP = 8
CAM = 12
LOG2E = 1.4426950408889634
VMEM_LIMIT = 56 * 1024 * 1024


def split3(value):
    high = value.astype(BF16).astype(F32)
    rest = value - high
    mid = rest.astype(BF16).astype(F32)
    return high, mid, rest - mid


def mm(left, right):
    return jnp.dot(left, right, preferred_element_type=F32)


def mm_t(left, right):
    return lax.dot_general(left, right, (((1,), (1,)), ((), ())), preferred_element_type=F32)


def pose_kernel(cam_ref, gain_ref, qkv_ref, out_ref, head_ref, cams_ref):
    cam = cam_ref[...].astype(F32)
    mean = jnp.mean(cam * cam, axis=-1, keepdims=True)
    normed = (cam * lax.rsqrt(mean + 1e-06) * gain_ref[...]).astype(BF16)
    query = mm(normed, qkv_ref[0]).astype(BF16)
    keys = mm(normed, qkv_ref[1]).astype(BF16)
    values = mm(normed, qkv_ref[2]).astype(BF16)
    mixed = []
    for head in range(HEADS):
        part = slice(head * HEAD_DIM, (head + 1) * HEAD_DIM)
        scores = mm_t(query[:, part], keys[:, part]) * (1.0 / HEAD_DIM**0.5)
        weights = jnp.exp(scores - jnp.max(scores, axis=-1, keepdims=True))
        total = jnp.sum(weights, axis=-1, keepdims=True)
        mixed.append((mm(weights.astype(BF16), values[:, part]) / total).astype(BF16))
    partial = mm(jnp.concatenate(mixed, axis=1), out_ref[...])
    cams_ref[...] = jnp.dot(
        partial + 0.5 * cam, head_ref[...], precision=lax.Precision.HIGHEST, preferred_element_type=F32
    )


def pose(cam_all, pose_norm, pose_qkv, pose_out, camera_head):
    return pl.pallas_call(
        pose_kernel,
        out_shape=jax.ShapeDtypeStruct((cam_all.shape[0], CAM), F32),
        compiler_params=pltpu.CompilerParams(vmem_limit_bytes=VMEM_LIMIT),
        name="pose",
    )(cam_all, pose_norm, pose_qkv, pose_out, camera_head)


def ray_rows(cams):
    frames = cams.shape[0]
    place_at = lax.broadcasted_iota(jnp.int32, (frames, ROWS), 1)
    across = ((place_at & (GRID - 1)).astype(F32) + 0.5) * (2.0 / GRID) - 1.0
    down = ((place_at >> 5).astype(F32) + 0.5) * (2.0 / GRID) - 1.0
    squashed = jnp.tanh(cams)

    def turn(which):
        return squashed[:, which : which + 1] * 0.3

    def place(which):
        return squashed[:, 9 + which : 10 + which] * 2.0

    one = (1.0 + turn(0)) * across + turn(1) * down + turn(2)
    two = turn(3) * across + (1.0 + turn(4)) * down + turn(5)
    three = turn(6) * across + turn(7) * down + (1.0 + turn(8))
    length = jnp.sqrt(one * one + two * two + three * three)
    u_one, u_two, u_three = one / length, two / length, three / length
    return (
        u_one,
        u_two,
        u_three,
        place(1) * u_three - place(2) * u_two,
        place(2) * u_one - place(0) * u_three,
        place(0) * u_two - place(1) * u_one,
    )


def prep_kernel(core_ref, cams_ref, embed_ref, gain_ref, qkv_ref, *refs):
    blocks, (q_ref, k_ref, v_ref, share_ref) = refs[:-4], refs[-4:]
    core = core_ref[0]
    other = 1 - core
    rays = ray_rows(cams_ref[...])
    zeros = jnp.zeros((2, ROWS), F32)
    jobs = [(0, blocks[0][...], blocks[1][...], 0, 0)]
    at = 2
    for step in range(1, GROUP):
        jobs.append((step, blocks[at][...], blocks[at + 1][...], step, None))
        at += 2
    jobs.append((GROUP + 4, blocks[at][...], blocks[at + 1][...], None, 4))
    at += 2
    for step in range(1, 4):
        for plane in range(2):
            jobs.append((GROUP + plane * 4 + step, blocks[at][plane], blocks[at + 1][plane], None, plane * 4 + step))
        at += 2
    for frame, near, far, key_at, query_at in jobs:
        six = jnp.concatenate([ray[frame : frame + 1] for ray in rays] + [zeros], axis=0)
        high, mid, low = split3(six)
        stacked = jnp.concatenate([high, high, mid, mid, high, low], axis=0).astype(BF16)

        def embedded(side):
            return lax.dot_general(
                stacked, embed_ref[side], (((0,), (0,)), ((), ())), preferred_element_type=F32
            )

        near_in = (near.astype(F32) + embedded(core)).astype(BF16)
        far_in = (far.astype(F32) + embedded(other)).astype(BF16)
        if frame == 0:
            share_ref[...] = near_in
        near_f = near_in.astype(F32)
        far_f = far_in.astype(F32)
        total = jnp.sum(near_f * near_f + far_f * far_f, axis=-1, keepdims=True)
        factor = lax.rsqrt(total * (1.0 / WIDTH) + 1e-06)
        near_n = (near_f * factor * gain_ref[core]).astype(BF16)
        far_n = (far_f * factor * gain_ref[other]).astype(BF16)

        def project(which):
            return mm(near_n, qkv_ref[which, core]) + mm(far_n, qkv_ref[which, other])

        if query_at is not None:
            q_ref[query_at] = (project(0) * (LOG2E / HEAD_DIM**0.5)).astype(BF16)
        if key_at is not None:
            span = pl.ds(key_at * ROWS, ROWS)
            k_ref[span, :] = project(1).astype(BF16)
            v_ref[span, :] = project(2).astype(BF16)


def prep(core, cams, embed, gain, qkv, blocks):
    smem = pl.BlockSpec(memory_space=pltpu.SMEM)
    vmem = pl.BlockSpec(memory_space=pltpu.VMEM)
    return pl.pallas_call(
        prep_kernel,
        in_specs=[smem] + [vmem] * (4 + len(blocks)),
        out_specs=[vmem] * 4,
        out_shape=[
            jax.ShapeDtypeStruct((GROUP, ROWS, HALF), BF16),
            jax.ShapeDtypeStruct((GROUP * ROWS, HALF), BF16),
            jax.ShapeDtypeStruct((GROUP * ROWS, HALF), BF16),
            jax.ShapeDtypeStruct((ROWS, HALF), BF16),
        ],
        compiler_params=pltpu.CompilerParams(vmem_limit_bytes=VMEM_LIMIT),
        name="prep",
    )(core, cams, embed, gain, qkv, *blocks)


def attend_kernel(q_ref, k_ref, v_ref, out_ref):
    keys_n = k_ref.shape[0]
    lane = lax.broadcasted_iota(jnp.int32, (1, 128), 1)
    ones = jnp.ones((keys_n, 128), BF16)
    stat = None
    for pair in range(PAIRS):
        part = slice(pair * 128, pair * 128 + 128)
        query = q_ref[0, :, part]
        keys = k_ref[:, part]
        values = v_ref[:, part]
        joined = None
        for side in range(2):
            mine = (lane >> 6) == side
            scores = mm_t(jnp.where(mine, query, jnp.zeros_like(query)), keys)
            top = jnp.max(scores, axis=-1, keepdims=True)
            weights = jnp.exp2(scores - top).astype(BF16)
            extended = jnp.concatenate([jnp.where(mine, values, jnp.zeros_like(values)), ones], axis=1)
            both = mm(weights, extended)
            total = both[:, 128:]
            result = both[:, :128] / total
            joined = result if joined is None else joined + result
            level = top + jnp.log2(total)
            head = pair * 2 + side
            stat = level if stat is None else jnp.where((lane & 7) == head, level, stat)
        out_ref[0, :, part] = joined.astype(BF16)
    high, mid, low = split3(stat)
    packed = jnp.where(lane < 8, high, jnp.where(lane < 16, mid, jnp.where(lane < 24, low, 0.0)))
    out_ref[0, :, HALF : HALF + 128] = packed.astype(BF16)


def attend(query, keys, values):
    count = query.shape[0]
    return pl.pallas_call(
        attend_kernel,
        grid=(count,),
        in_specs=[
            pl.BlockSpec((1, ROWS, HALF), lambda i: (i, 0, 0)),
            pl.BlockSpec(memory_space=pltpu.VMEM),
            pl.BlockSpec(memory_space=pltpu.VMEM),
        ],
        out_specs=pl.BlockSpec((1, ROWS, HALF + 128), lambda i: (i, 0, 0)),
        out_shape=jax.ShapeDtypeStruct((count, ROWS, HALF + 128), BF16),
        compiler_params=pltpu.CompilerParams(vmem_limit_bytes=VMEM_LIMIT),
        name="attend",
    )(query, keys, values)


def merge_kernel(core_ref, out_ref, *refs):
    parts, (mine_ref, send_ref) = refs[:-2], refs[-2:]
    core = core_ref[0]
    row = lax.broadcasted_iota(jnp.int32, (128, HALF), 0)
    column = lax.broadcasted_iota(jnp.int32, (128, HALF), 1)
    spread = jnp.where(((row & 7) == (column >> 6)) & (row < 24), 1.0, 0.0).astype(BF16)
    levels = [mm(part[0, :, HALF:], spread) for part in parts]
    top = levels[0]
    for level in levels[1:]:
        top = jnp.maximum(top, level)
    total = None
    mixed = None
    for part, level in zip(parts, levels):
        weight = jnp.exp2(level - top)
        value = weight * part[0, :, :HALF].astype(F32)
        total = weight if total is None else total + weight
        mixed = value if mixed is None else mixed + value
    attended = (mixed / total).astype(BF16)
    mine_ref[...] = mm(attended, out_ref[:, pl.ds(pl.multiple_of(core * HALF, HALF), HALF)])
    send_ref[...] = mm(attended, out_ref[:, pl.ds(pl.multiple_of((1 - core) * HALF, HALF), HALF)]).astype(BF16)


def merge(core, render_out, parts):
    smem = pl.BlockSpec(memory_space=pltpu.SMEM)
    vmem = pl.BlockSpec(memory_space=pltpu.VMEM)
    return pl.pallas_call(
        merge_kernel,
        in_specs=[smem, vmem] + [vmem] * len(parts),
        out_specs=[vmem] * 2,
        out_shape=[
            jax.ShapeDtypeStruct((ROWS, HALF), F32),
            jax.ShapeDtypeStruct((ROWS, HALF), BF16),
        ],
        compiler_params=pltpu.CompilerParams(vmem_limit_bytes=VMEM_LIMIT),
        name="merge",
    )(core, render_out, *parts)


def shift(value, axis, size, by):
    return lax.ppermute(value, axis, [(at, (at + by) % size) for at in range(size)])


def shift_xy(value, by_x, by_y):
    pairs = [
        (x * 2 + y, ((x + by_x) % 4) * 2 + (y + by_y) % 2) for x in range(4) for y in range(2)
    ]
    return lax.ppermute(value, ("x", "y"), pairs)


def local(
    tokens,
    frame_order,
    target_mask,
    pose_norm,
    pose_qkv,
    pose_out,
    camera_head,
    ray_embed,
    render_norm,
    render_qkv,
    render_out,
):
    core = lax.axis_index("h")
    core_arr = core.astype(jnp.int32).reshape(1)
    pooled = jnp.mean(tokens, axis=0, dtype=F32)[None, :]
    rate = jnp.exp(-4.0 * jnp.arange(WIDTH, dtype=F32) / WIDTH)
    cam_in = (pooled + jnp.sin(frame_order.astype(F32)[:, None] * rate[None, :])).astype(BF16)

    gathered = cam_in.reshape(1, 8, 128)
    gathered = jnp.concatenate([gathered] + [shift(gathered, "x", 4, by) for by in (1, 2, 3)], axis=0)
    gathered = jnp.concatenate([gathered, shift(gathered, "y", 2, 1)], axis=0)
    gathered = jnp.concatenate([gathered] + [shift(gathered, "z", 8, by) for by in range(1, 8)], axis=0)
    cam_all = gathered.reshape(64, WIDTH)

    kept = tokens * (1 - target_mask).astype(BF16)[:, None]
    near = lax.dynamic_slice_in_dim(kept, core * HALF, HALF, 1)
    far = lax.dynamic_slice_in_dim(kept, (1 - core) * HALF, HALF, 1)

    def both(value):
        return [value, shift(value, "h", 2, 1)]

    blocks = [near, far]
    up, down = near, near
    ring = {}
    for step in range(1, 5):
        up = shift(up, "z", 8, 1)
        ring[step] = up
        if step < 4:
            down = shift(down, "z", 8, 7)
            ring[8 - step] = down
    for step in range(1, 8):
        blocks += both(ring[step])
    across = shift(near, "y", 2, 1)
    planes = jnp.stack([near, across])
    blocks += both(across)
    for step in (1, 2, 3):
        blocks += both(shift(planes, "x", 4, step))

    cams = pose(cam_all, pose_norm[None, :], pose_qkv, pose_out, camera_head)
    cams = cams + shift(cams, "h", 2, 1)
    group_cams = jnp.concatenate([cams[0:64:8], cams[0:8]], axis=0)

    high, mid, low = split3(jnp.pad(ray_embed, ((0, 2), (0, 0))))
    embed = jnp.concatenate([high, mid, high, mid, low, high], axis=0).astype(BF16)
    embed = embed.reshape(48, 2, HALF).transpose(1, 0, 2)
    query, keys, values, share = prep(
        core_arr,
        group_cams,
        embed,
        render_norm.reshape(2, 1, HALF),
        render_qkv.reshape(3, 2, HALF, HALF),
        blocks,
    )
    parts = attend(query, keys, values)
    received = [parts[0:1]]
    for at in range(1, 8):
        by_x, by_y = at % 4, at // 4
        received.append(shift_xy(parts[at : at + 1], -by_x, -by_y))
    mine, send = merge(core_arr, render_out, received)
    theirs = shift(send, "h", 2, 1)
    rendered = (share.astype(F32) + (mine + theirs.astype(F32))).astype(BF16)
    return (rendered, cams[0:1])


def solution(mesh):
    fine = Mesh(mesh.devices.reshape(4, 2, 8, 2, 2), ("x", "y", "z", "h", "dp"))
    rows = ("dp", "x", "y", "z")
    in_specs = (
        P(rows, None),
        P(rows),
        P(rows),
        P(),
        P(None, None, "h"),
        P("h", None),
        P(),
        P(),
        P(),
        P(None, None, "h"),
        P("h", None),
    )
    out_specs = (P(rows, "h"), P(rows, None))
    return jax.shard_map(local, mesh=fine, in_specs=in_specs, out_specs=out_specs, check_vma=False)
```

```python
import functools

import jax
import jax.numpy as jnp
from jax import lax
from jax.experimental import pallas as pl
from jax.experimental.pallas import tpu as pltpu
from jax.sharding import Mesh
from jax.sharding import PartitionSpec as P

F32 = jnp.float32
BF16 = jnp.bfloat16
HEAD_DIM = 64
GRID = 32
ROWS = 192
WIDTH = 1024
HALF = 512
HEADS = 8
PAIRS = 4
GROUP = 8
RING = 4
TALL = 208
CAM = 12
FRAMES = 64
LOG2E = 1.4426950408889634
VMEM_LIMIT = 56 * 1024 * 1024
SMEM = pl.BlockSpec(memory_space=pltpu.SMEM)
VMEM = pl.BlockSpec(memory_space=pltpu.VMEM)


def split3(value):
    high = value.astype(BF16).astype(F32)
    rest = value - high
    mid = rest.astype(BF16).astype(F32)
    return high, mid, rest - mid


def mm(left, right):
    return jnp.dot(left, right, preferred_element_type=F32)


def mm_t(left, right):
    return lax.dot_general(left, right, (((1,), (1,)), ((), ())), preferred_element_type=F32)


def start_kernel(order_ref, mask_ref, tokens_ref, send_ref, near_ref, far_ref):
    tokens = tokens_ref[...].astype(F32)
    pooled = jnp.sum(tokens, axis=0, keepdims=True) * (1.0 / ROWS)
    pieces = [pooled[:, at * 128 : at * 128 + 128] for at in range(8)]
    index = lax.broadcasted_iota(jnp.int32, (8, 128), 0) * 128 + lax.broadcasted_iota(jnp.int32, (8, 128), 1)
    rate = jnp.exp(-4.0 * index.astype(F32) / WIDTH)
    wave = jnp.sin(order_ref[0].astype(F32) * rate)
    cam = (jnp.concatenate(pieces, axis=0) + wave).astype(BF16).astype(F32)
    send_ref[...] = jnp.broadcast_to(cam[None], send_ref.shape)
    kept = (tokens * (1 - mask_ref[0]).astype(F32)).astype(BF16)
    first = lax.axis_index("h") == 0
    near_ref[...] = jnp.where(first, kept[:, :HALF], kept[:, HALF:])
    far_ref[...] = jnp.where(first, kept[:, HALF:], kept[:, :HALF])


def start(order, mask, tokens):
    return pl.pallas_call(
        start_kernel,
        in_specs=[SMEM, SMEM, VMEM],
        out_specs=[VMEM] * 3,
        out_shape=[
            jax.ShapeDtypeStruct((FRAMES, 8, 128), F32),
            jax.ShapeDtypeStruct((ROWS, HALF), BF16),
            jax.ShapeDtypeStruct((ROWS, HALF), BF16),
        ],
        compiler_params=pltpu.CompilerParams(vmem_limit_bytes=VMEM_LIMIT),
        name="start",
    )(order, mask, tokens)


def pose_kernel(cam_ref, gain_ref, qkv_ref, out_ref, head_ref, cams_ref):
    cam = jnp.concatenate([cam_ref[:, at, :] for at in range(8)], axis=1)
    mean = jnp.mean(cam * cam, axis=-1, keepdims=True)
    normed = (cam * lax.rsqrt(mean + 1e-06) * gain_ref[...]).astype(BF16)
    query = mm(normed, qkv_ref[0]).astype(BF16)
    keys = mm(normed, qkv_ref[1]).astype(BF16)
    values = mm(normed, qkv_ref[2]).astype(BF16)
    lane_head = lax.broadcasted_iota(jnp.int32, (FRAMES, HALF), 1) >> 6
    stacked = jnp.concatenate(
        [jnp.where(lane_head == head, query, jnp.zeros_like(query)) for head in range(HEADS)], axis=0
    )
    scores = mm_t(stacked, keys) * (1.0 / HEAD_DIM**0.5)
    weights = jnp.exp(scores - jnp.max(scores, axis=-1, keepdims=True))
    total = jnp.sum(weights, axis=-1, keepdims=True)
    mixed = mm(weights.astype(BF16), values) / total
    picked = None
    for head in range(HEADS):
        rows = mixed[head * FRAMES : (head + 1) * FRAMES]
        picked = rows if picked is None else jnp.where(lane_head == head, rows, picked)
    partial = mm(picked.astype(BF16), out_ref[...]) + 0.5 * cam
    cams_ref[...] = lax.dot_general(
        partial,
        head_ref[...],
        (((1,), (1,)), ((), ())),
        precision=lax.Precision.HIGHEST,
        preferred_element_type=F32,
    )


def pose(cam_all, pose_norm, pose_qkv, pose_out, camera_head):
    return pl.pallas_call(
        pose_kernel,
        out_shape=jax.ShapeDtypeStruct((FRAMES, CAM), F32),
        compiler_params=pltpu.CompilerParams(vmem_limit_bytes=VMEM_LIMIT),
        name="pose",
    )(cam_all, pose_norm, pose_qkv, pose_out, camera_head)


def ray_rows(cams):
    frames = cams.shape[0]
    place_at = lax.broadcasted_iota(jnp.int32, (frames, ROWS), 1)
    across = ((place_at & (GRID - 1)).astype(F32) + 0.5) * (2.0 / GRID) - 1.0
    down = ((place_at >> 5).astype(F32) + 0.5) * (2.0 / GRID) - 1.0
    squashed = jnp.tanh(cams)

    def turn(which):
        return squashed[:, which : which + 1] * 0.3

    def place(which):
        return squashed[:, 9 + which : 10 + which] * 2.0

    one = (1.0 + turn(0)) * across + turn(1) * down + turn(2)
    two = turn(3) * across + (1.0 + turn(4)) * down + turn(5)
    three = turn(6) * across + turn(7) * down + (1.0 + turn(8))
    length = jnp.sqrt(one * one + two * two + three * three)
    u_one, u_two, u_three = one / length, two / length, three / length
    return (
        u_one,
        u_two,
        u_three,
        place(1) * u_three - place(2) * u_two,
        place(2) * u_one - place(0) * u_three,
        place(0) * u_two - place(1) * u_one,
    )


def prep_kernel(keys, queries, spots, place_ref, cams_ref, more_ref, embed_ref, gain_ref, qkv_hbm, *refs):
    frames = [("k", offset) for group in keys for offset in group] + [("q",) + spot for group in queries for spot in group]
    arrays = 2 * (max(spot[0] for spot in spots) + 1)
    inputs = refs[:arrays]
    outputs = list(refs[arrays:-4])
    qkv_ref, near_buf, far_buf, sems = refs[-4:]
    at_x, at_y, at_z, core = (place_ref[at] for at in range(4))
    other = 1 - core
    copies = []

    def fetch(source, target):
        copy = pltpu.make_async_copy(source, target, sems.at[len(copies)])
        copy.start()
        copies.append(copy)
        return copy

    matrices = ([1, 2] if keys else []) + ([0] if queries else [])
    weights = {which: fetch(qkv_hbm.at[which], qkv_ref.at[which]) for which in matrices}
    waits = []
    for at, (array, plane) in enumerate(spots):
        pair = inputs[2 * array : 2 * array + 2]
        if plane is not None:
            pair = [ref.at[plane] for ref in pair]
        waits.append([fetch(pair[0], near_buf.at[at]), fetch(pair[1], far_buf.at[at])])
    row = lax.broadcasted_iota(jnp.int32, (2 * GROUP, FRAMES), 0)
    key_frame = at_x * 16 + at_y * 8 + ((at_z - row) & 7)
    query_frame = ((at_x - row) & 3) * 16 + ((at_y - (row >> 2)) & 1) * 8 + at_z
    wanted = jnp.where(row < GROUP, key_frame, query_frame)
    pick = jnp.where(lax.broadcasted_iota(jnp.int32, (2 * GROUP, FRAMES), 1) == wanted, 1.0, 0.0)
    cams = jnp.dot(
        pick, cams_ref[...] + more_ref[...], precision=lax.Precision.HIGHEST, preferred_element_type=F32
    )
    rays = ray_rows(cams)
    zeros = jnp.zeros((2, ROWS), F32)
    embeds = []
    for side in (core, other):
        pad = jnp.zeros((2, HALF), F32)
        span = pl.ds(pl.multiple_of(side * HALF, HALF), HALF)
        high, mid, low = split3(jnp.concatenate([embed_ref[:, span], pad], axis=0))
        embeds.append(jnp.concatenate([high, mid, high, mid, low, high], axis=0).astype(BF16))

    def inputs_of(at):
        kind = frames[at]
        frame = kind[1] if kind[0] == "k" else GROUP + kind[2] * RING + kind[1]
        six = jnp.concatenate([ray[frame : frame + 1] for ray in rays] + [zeros], axis=0)
        high, mid, low = split3(six)
        stacked = jnp.concatenate([high, high, mid, mid, high, low], axis=0).astype(BF16)

        def embedded(side):
            return lax.dot_general(
                stacked, embeds[side], (((0,), (0,)), ((), ())), preferred_element_type=F32
            )

        near_in = (near_buf[at].astype(F32) + embedded(0)).astype(BF16)
        far_in = (far_buf[at].astype(F32) + embedded(1)).astype(BF16)
        return near_in, far_in

    def normed(pair):
        near_f = pair[0].astype(F32)
        far_f = pair[1].astype(F32)
        total = jnp.sum(near_f * near_f + far_f * far_f, axis=-1, keepdims=True)
        factor = lax.rsqrt(total * (1.0 / WIDTH) + 1e-06)
        return (near_f * factor * gain_ref[core]).astype(BF16), (far_f * factor * gain_ref[other]).astype(BF16)

    def project(pair, which):
        return mm(pair[0], qkv_ref[which, core]) + mm(pair[1], qkv_ref[which, other])

    def stacked_of(parts):
        return tuple(jnp.concatenate([part[side] for part in parts], axis=0) for side in range(2))

    if keys:
        k_ref, v_ref = outputs[:2]
        outputs = outputs[2:]
    if queries:
        q_ref, share_ref, own_ref = outputs
        own_ref[...] = cams[0:1]
    at = 0
    for group in list(keys) + list(queries):
        members = range(at, at + len(group))
        for member in members:
            for copy in waits[member]:
                copy.wait()
        raw = [inputs_of(member) for member in members]
        pair = stacked_of([normed(part) for part in raw])
        if frames[at][0] == "k":
            if at == 0:
                for which in (1, 2):
                    weights[which].wait()
            span = slice(at * ROWS, (at + len(group)) * ROWS)
            k_ref[span, :] = project(pair, 1).astype(BF16)
            v_ref[span, :] = project(pair, 2).astype(BF16)
        else:
            if group is queries[0]:
                weights[0].wait()
            query = (project(pair, 0) * (LOG2E / HEAD_DIM**0.5)).astype(BF16)
            for spot, (by_x, by_y) in enumerate(group):
                if (by_x, by_y) == (0, 0):
                    share_ref[...] = raw[spot][0]
                q_ref[by_y * RING + ((at_x - by_x) & (RING - 1))] = query[spot * ROWS : (spot + 1) * ROWS]
        at += len(group)


def prep(keys, queries, place, cams, more, embed, gain, qkv, blocks):
    any_space = pl.BlockSpec(memory_space=pltpu.HBM)
    spots = []
    for array, value in enumerate(blocks):
        spots += [(array, None)] if value[0].ndim == 2 else [(array, plane) for plane in range(2)]
    count = len(spots)
    blocks = [item for value in blocks for item in value]
    shapes = []
    if keys:
        shapes += [jax.ShapeDtypeStruct((sum(len(group) for group in keys) * ROWS, HALF), BF16)] * 2
    if queries:
        shapes += [
            jax.ShapeDtypeStruct((GROUP, ROWS, HALF), BF16),
            jax.ShapeDtypeStruct((ROWS, HALF), BF16),
            jax.ShapeDtypeStruct((1, CAM), F32),
        ]
    return pl.pallas_call(
        functools.partial(prep_kernel, keys, queries, tuple(spots)),
        in_specs=[SMEM, VMEM, VMEM, VMEM, VMEM, any_space] + [any_space] * len(blocks),
        out_specs=[VMEM] * len(shapes),
        out_shape=shapes,
        scratch_shapes=[
            pltpu.VMEM((3, 2, HALF, HALF), BF16),
            pltpu.VMEM((count, ROWS, HALF), BF16),
            pltpu.VMEM((count, ROWS, HALF), BF16),
            pltpu.SemaphoreType.DMA((2 * count + 3,)),
        ],
        compiler_params=pltpu.CompilerParams(vmem_limit_bytes=VMEM_LIMIT),
        name="prep",
    )(place, cams, more, embed, gain, qkv, *blocks)


def pack_levels(out_ref, index, compact):
    out_ref[index, ROWS:TALL, :] = jnp.zeros((TALL - ROWS, HALF), BF16)
    out_ref[index, ROWS:TALL, 0:ROWS] = compact[0:16].astype(BF16)
    out_ref[index, ROWS:TALL, 256 : 256 + ROWS] = compact[16:32].astype(BF16)


def attend_kernel(pieces, q_ref, *refs):
    k_refs, v_refs, out_ref = refs[:pieces], refs[pieces : 2 * pieces], refs[-1]
    lane = lax.broadcasted_iota(jnp.int32, (1, 128), 1)
    count = q_ref.shape[0]
    stat = None
    for pair in range(PAIRS):
        part = slice(pair * 128, pair * 128 + 128)
        query = jnp.concatenate([q_ref[at, :, part] for at in range(count)], axis=0)
        keys = jnp.concatenate([ref[:, part] for ref in k_refs], axis=0)
        values = jnp.concatenate([ref[:, part] for ref in v_refs], axis=0)
        ones = jnp.ones((keys.shape[0], 128), BF16)
        joined = None
        for side in range(2):
            mine = (lane >> 6) == side
            scores = mm_t(jnp.where(mine, query, jnp.zeros_like(query)), keys)
            top = jnp.max(scores, axis=-1, keepdims=True)
            weights = jnp.exp2(scores - top).astype(BF16)
            extended = jnp.concatenate([jnp.where(mine, values, jnp.zeros_like(values)), ones], axis=1)
            both = mm(weights, extended)
            total = both[:, 128:]
            result = both[:, :128] / total
            joined = result if joined is None else joined + result
            level = top + jnp.log2(total)
            head = pair * 2 + side
            stat = level if stat is None else jnp.where((lane & 7) == head, level, stat)
        joined = joined.astype(BF16)
        for at in range(count):
            out_ref[at, 0:ROWS, part] = joined[at * ROWS : (at + 1) * ROWS]
    high, mid, low = split3(stat)
    packed = jnp.where(lane < 8, high, jnp.where(lane < 16, mid, jnp.where(lane < 24, low, 0.0))).astype(BF16)
    same = lax.broadcasted_iota(jnp.int32, (32, 128), 0) == lax.broadcasted_iota(jnp.int32, (32, 128), 1)
    pick = jnp.where(same, 1.0, 0.0).astype(BF16)
    for at in range(count):
        pack_levels(out_ref, at, mm_t(pick, packed[at * ROWS : (at + 1) * ROWS]))


def attend(query, keys, values, plane):
    return pl.pallas_call(
        functools.partial(attend_kernel, len(keys)),
        grid=(RING // 2,),
        in_specs=[pl.BlockSpec((2, ROWS, HALF), lambda i: (plane * 2 + i, 0, 0))]
        + [VMEM] * (2 * len(keys)),
        out_specs=pl.BlockSpec((2, TALL, HALF), lambda i: (i, 0, 0)),
        out_shape=jax.ShapeDtypeStruct((RING, TALL, HALF), BF16),
        compiler_params=pltpu.CompilerParams(vmem_limit_bytes=VMEM_LIMIT),
        name="attend",
    )(query, *keys, *values)


def join_parts(parts):
    row = lax.broadcasted_iota(jnp.int32, (32, HALF), 0)
    column = lax.broadcasted_iota(jnp.int32, (32, HALF), 1)
    spread = jnp.where(((row & 7) == (column >> 6)) & (row < 24), 1.0, 0.0).astype(BF16)
    levels = []
    for ref, index in parts:
        compact = jnp.concatenate(
            [ref[index, ROWS:TALL, 0:ROWS], ref[index, ROWS:TALL, 256 : 256 + ROWS]], axis=0
        )
        levels.append(
            lax.dot_general(compact, spread, (((0,), (0,)), ((), ())), preferred_element_type=F32)
        )
    top = levels[0]
    for level in levels[1:]:
        top = jnp.maximum(top, level)
    total = None
    mixed = None
    for (ref, index), level in zip(parts, levels):
        weight = jnp.exp2(level - top)
        value = weight * ref[index, 0:ROWS, :].astype(F32)
        total = weight if total is None else total + weight
        mixed = value if mixed is None else mixed + value
    return mixed / total, top, total


def join_kernel(parts_ref, out_ref):
    result, top, total = join_parts([(parts_ref, at) for at in range(RING)])
    out_ref[0, 0:ROWS, :] = result.astype(BF16)
    row = lax.broadcasted_iota(jnp.int32, (8, HALF), 0)
    column = lax.broadcasted_iota(jnp.int32, (8, HALF), 1)
    pick = jnp.where(row * HEAD_DIM == column, 1.0, 0.0).astype(BF16)
    pieces = [mm_t(pick, piece.astype(BF16)) for piece in split3(top + jnp.log2(total))]
    pack_levels(out_ref, 0, jnp.concatenate(pieces + [jnp.zeros((8, ROWS), F32)], axis=0))


def join(parts):
    return pl.pallas_call(
        join_kernel,
        out_shape=jax.ShapeDtypeStruct((1, TALL, HALF), BF16),
        compiler_params=pltpu.CompilerParams(vmem_limit_bytes=VMEM_LIMIT),
        name="join",
    )(parts)


def merge_kernel(place_ref, out_ref, parts_ref, more_ref, mine_ref, send_ref):
    core = place_ref[3]
    result, _, _ = join_parts([(parts_ref, at) for at in range(RING)] + [(more_ref, 0)])
    attended = result.astype(BF16)
    mine_ref[...] = mm(attended, out_ref[:, pl.ds(pl.multiple_of(core * HALF, HALF), HALF)])
    send_ref[...] = mm(attended, out_ref[:, pl.ds(pl.multiple_of((1 - core) * HALF, HALF), HALF)]).astype(BF16)


def merge(place, render_out, parts, more):
    return pl.pallas_call(
        merge_kernel,
        in_specs=[SMEM, VMEM, VMEM, VMEM],
        out_specs=[VMEM] * 2,
        out_shape=[
            jax.ShapeDtypeStruct((ROWS, HALF), F32),
            jax.ShapeDtypeStruct((ROWS, HALF), BF16),
        ],
        compiler_params=pltpu.CompilerParams(vmem_limit_bytes=VMEM_LIMIT),
        name="merge",
    )(place, render_out, parts, more)


def shift(value, axis, size, by):
    return lax.ppermute(value, axis, [(at, (at + by) % size) for at in range(size)])


def local(
    tokens,
    frame_order,
    target_mask,
    pose_norm,
    pose_qkv,
    pose_out,
    camera_head,
    ray_embed,
    render_norm,
    render_qkv,
    render_out,
):
    at_x, at_y, at_z, core = (lax.axis_index(name) for name in ("x", "y", "z", "h"))
    place = jnp.stack([at_x, at_y, at_z, core]).astype(jnp.int32)
    send, near, far = start(frame_order, target_mask, tokens)

    def other(value):
        return shift(value, "h", 2, 1)

    def step_up(value):
        return shift(value, "z", 8, 1)

    def step_down(value):
        return shift(value, "z", 8, 7)

    tie = lax.optimization_barrier
    cam_all = lax.all_to_all(send, ("x", "y", "z"), 0, 0)
    up1, down1, across = step_up(near), step_down(near), shift(near, "y", 2, 1)
    opposite = shift(near, "z", 8, 4)
    cam_all, up1, down1, across = tie((cam_all, up1, down1, across))
    up2, down2 = step_up(up1), step_down(down1)
    planes = jnp.stack([near, across])
    side1, side3, side2 = (shift(planes, "x", 4, by) for by in (1, 3, 2))
    cams = pose(cam_all, pose_norm[None, :], pose_qkv, pose_out, camera_head.T)
    cams, up2, down2 = tie((cams, up2, down2))
    more = other(cams)
    up3, down3 = step_up(up2), step_down(down2)
    more, up3, down3, side1, side3, side2, opposite = tie((more, up3, down3, side1, side3, side2, opposite))
    gain = render_norm.reshape(2, 1, HALF)
    qkv = render_qkv.reshape(3, 2, HALF, HALF)

    def pair(value):
        return (value, other(value))

    own_pair = (near, far)
    key, val, query, share, own = prep(
        ((0, 1, 7, 2), (6, 4, 3, 5)),
        (((0, 0), (0, 1)), ((1, 0), (1, 1), (3, 0), (3, 1)), ((2, 0), (2, 1))),
        place,
        cams,
        more,
        ray_embed,
        gain,
        qkv,
        [own_pair]
        + [pair(value) for value in (up1, down1, up2, down2, opposite, up3, down3)]
        + [own_pair]
        + [pair(value) for value in (across, side1, side3, side2)],
    )
    keys, values = (key,), (val,)
    far_parts = lax.all_to_all(attend(query, keys, values, 1), "x", 0, 0)
    near_parts = lax.all_to_all(attend(query, keys, values, 0), "x", 0, 0)
    crossed = shift(join(far_parts), "y", 2, 1)
    mine, outgoing = merge(place, render_out, near_parts, crossed)
    theirs = other(outgoing)
    rendered = (share.astype(F32) + (mine + theirs.astype(F32))).astype(BF16)
    return (rendered, own)


def solution(mesh):
    fine = Mesh(mesh.devices.reshape(4, 2, 8, 2, 2), ("x", "y", "z", "h", "dp"))
    rows = ("dp", "x", "y", "z")
    in_specs = (
        P(rows, None),
        P(rows),
        P(rows),
        P(),
        P(None, None, "h"),
        P("h", None),
        P(),
        P(),
        P(),
        P(None, None, "h"),
        P("h", None),
    )
    out_specs = (P(rows, "h"), P(rows, None))
    return jax.shard_map(local, mesh=fine, in_specs=in_specs, out_specs=out_specs, check_vma=False)
```

```python
import functools

import jax
import jax.numpy as jnp
from jax import lax
from jax.experimental import pallas as pl
from jax.experimental.pallas import tpu as pltpu
from jax.sharding import Mesh
from jax.sharding import PartitionSpec as P

F32 = jnp.float32
BF16 = jnp.bfloat16
HEAD_DIM = 64
GRID = 32
ROWS = 192
WIDTH = 1024
HALF = 512
HEADS = 8
PAIRS = 4
GROUP = 8
RING = 4
TALL = 208
CAM = 12
FRAMES = 64
LOG2E = 1.4426950408889634
VMEM_LIMIT = 56 * 1024 * 1024
SMEM = pl.BlockSpec(memory_space=pltpu.SMEM)
VMEM = pl.BlockSpec(memory_space=pltpu.VMEM)


def split3(value):
    high = value.astype(BF16).astype(F32)
    rest = value - high
    mid = rest.astype(BF16).astype(F32)
    return high, mid, rest - mid


def mm(left, right):
    return jnp.dot(left, right, preferred_element_type=F32)


def mm_t(left, right):
    return lax.dot_general(left, right, (((1,), (1,)), ((), ())), preferred_element_type=F32)


def start_kernel(order_ref, mask_ref, tokens_ref, send_ref, near_ref, far_ref):
    tokens = tokens_ref[...].astype(F32)
    pooled = jnp.sum(tokens, axis=0, keepdims=True) * (1.0 / ROWS)
    pieces = [pooled[:, at * 128 : at * 128 + 128] for at in range(8)]
    index = lax.broadcasted_iota(jnp.int32, (8, 128), 0) * 128 + lax.broadcasted_iota(jnp.int32, (8, 128), 1)
    rate = jnp.exp(-4.0 * index.astype(F32) / WIDTH)
    wave = jnp.sin(order_ref[0].astype(F32) * rate)
    cam = (jnp.concatenate(pieces, axis=0) + wave).astype(BF16).astype(F32)
    send_ref[...] = jnp.broadcast_to(cam[None], send_ref.shape)
    kept = (tokens * (1 - mask_ref[0]).astype(F32)).astype(BF16)
    first = lax.axis_index("h") == 0
    near_ref[...] = jnp.where(first, kept[:, :HALF], kept[:, HALF:])
    far_ref[...] = jnp.where(first, kept[:, HALF:], kept[:, :HALF])


def start(order, mask, tokens):
    return pl.pallas_call(
        start_kernel,
        in_specs=[SMEM, SMEM, VMEM],
        out_specs=[VMEM] * 3,
        out_shape=[
            jax.ShapeDtypeStruct((FRAMES, 8, 128), F32),
            jax.ShapeDtypeStruct((ROWS, HALF), BF16),
            jax.ShapeDtypeStruct((ROWS, HALF), BF16),
        ],
        compiler_params=pltpu.CompilerParams(vmem_limit_bytes=VMEM_LIMIT),
        name="start",
    )(order, mask, tokens)


def pose_kernel(cam_ref, gain_ref, qkv_ref, out_ref, head_ref, cams_ref):
    cam = jnp.concatenate([cam_ref[:, at, :] for at in range(8)], axis=1)
    mean = jnp.mean(cam * cam, axis=-1, keepdims=True)
    normed = (cam * lax.rsqrt(mean + 1e-06) * gain_ref[...]).astype(BF16)
    query = mm(normed, qkv_ref[0]).astype(BF16)
    keys = mm(normed, qkv_ref[1]).astype(BF16)
    values = mm(normed, qkv_ref[2]).astype(BF16)
    lane_head = lax.broadcasted_iota(jnp.int32, (FRAMES, HALF), 1) >> 6
    stacked = jnp.concatenate(
        [jnp.where(lane_head == head, query, jnp.zeros_like(query)) for head in range(HEADS)], axis=0
    )
    scores = mm_t(stacked, keys) * (1.0 / HEAD_DIM**0.5)
    weights = jnp.exp(scores - jnp.max(scores, axis=-1, keepdims=True))
    total = jnp.sum(weights, axis=-1, keepdims=True)
    mixed = mm(weights.astype(BF16), values) / total
    picked = None
    for head in range(HEADS):
        rows = mixed[head * FRAMES : (head + 1) * FRAMES]
        picked = rows if picked is None else jnp.where(lane_head == head, rows, picked)
    partial = mm(picked.astype(BF16), out_ref[...]) + 0.5 * cam
    cams_ref[...] = lax.dot_general(
        partial,
        head_ref[...],
        (((1,), (1,)), ((), ())),
        precision=lax.Precision.HIGHEST,
        preferred_element_type=F32,
    )


def pose(cam_all, pose_norm, pose_qkv, pose_out, camera_head):
    return pl.pallas_call(
        pose_kernel,
        out_shape=jax.ShapeDtypeStruct((FRAMES, CAM), F32),
        compiler_params=pltpu.CompilerParams(vmem_limit_bytes=VMEM_LIMIT),
        name="pose",
    )(cam_all, pose_norm, pose_qkv, pose_out, camera_head)


def ray_rows(cams):
    frames = cams.shape[0]
    place_at = lax.broadcasted_iota(jnp.int32, (frames, ROWS), 1)
    across = ((place_at & (GRID - 1)).astype(F32) + 0.5) * (2.0 / GRID) - 1.0
    down = ((place_at >> 5).astype(F32) + 0.5) * (2.0 / GRID) - 1.0
    squashed = jnp.tanh(cams)

    def turn(which):
        return squashed[:, which : which + 1] * 0.3

    def place(which):
        return squashed[:, 9 + which : 10 + which] * 2.0

    one = (1.0 + turn(0)) * across + turn(1) * down + turn(2)
    two = turn(3) * across + (1.0 + turn(4)) * down + turn(5)
    three = turn(6) * across + turn(7) * down + (1.0 + turn(8))
    length = jnp.sqrt(one * one + two * two + three * three)
    u_one, u_two, u_three = one / length, two / length, three / length
    return (
        u_one,
        u_two,
        u_three,
        place(1) * u_three - place(2) * u_two,
        place(2) * u_one - place(0) * u_three,
        place(0) * u_two - place(1) * u_one,
    )


def prep_kernel(keys, queries, spots, cams_ref, more_ref, embed_ref, gain_ref, qkv_hbm, *refs):
    frames = [("k", offset) for group in keys for offset in group] + [("q",) + spot for group in queries for spot in group]
    arrays = 2 * (max(spot[0] for spot in spots) + 1)
    inputs = refs[:arrays]
    k_hbm, v_hbm, q_hbm, share_ref, own_ref = refs[arrays : arrays + 5]
    qkv_ref, block_buf, k_ref, v_ref, q_ref, sems, out_sems = refs[arrays + 5 :]
    sent = []

    def send(source, target):
        copy = pltpu.make_async_copy(source, target, out_sems.at[len(sent)])
        copy.start()
        sent.append(copy)

    at_x, at_y, at_z, core = (lax.axis_index(name) for name in ("x", "y", "z", "h"))
    other = 1 - core
    copies = []

    def fetch(source, target):
        copy = pltpu.make_async_copy(source, target, sems.at[len(copies)])
        copy.start()
        copies.append(copy)
        return copy

    matrices = ([1, 2] if keys else []) + ([0] if queries else [])
    weights = {
        which: [
            fetch(qkv_hbm.at[which, side], qkv_ref.at[which, pl.ds(at * HALF, HALF)])
            for at, side in enumerate((core, other))
        ]
        for which in matrices
    }
    waits = []
    for at, (array, plane) in enumerate(spots):
        pair = inputs[2 * array : 2 * array + 2]
        if plane is not None:
            pair = [ref.at[plane] for ref in pair]
        waits.append(
            [fetch(ref, block_buf.at[at, :, pl.ds(side * HALF, HALF)]) for side, ref in enumerate(pair)]
        )
    row = lax.broadcasted_iota(jnp.int32, (2 * GROUP, FRAMES), 0)
    key_frame = at_x * 16 + at_y * 8 + ((at_z - row) & 7)
    query_frame = ((at_x - row) & 3) * 16 + ((at_y - (row >> 2)) & 1) * 8 + at_z
    wanted = jnp.where(row < GROUP, key_frame, query_frame)
    pick = jnp.where(lax.broadcasted_iota(jnp.int32, (2 * GROUP, FRAMES), 1) == wanted, 1.0, 0.0)
    cams = jnp.dot(
        pick, cams_ref[...] + more_ref[...], precision=lax.Precision.HIGHEST, preferred_element_type=F32
    )
    rays = ray_rows(cams)
    zeros = jnp.zeros((2, ROWS), F32)
    embeds = []
    for side in (core, other):
        pad = jnp.zeros((2, HALF), F32)
        span = pl.ds(pl.multiple_of(side * HALF, HALF), HALF)
        high, mid, low = split3(jnp.concatenate([embed_ref[:, span], pad], axis=0))
        embeds.append(jnp.concatenate([high, mid, high, mid, low, high], axis=0).astype(BF16))
    embeds = jnp.concatenate(embeds, axis=1)
    gains = jnp.concatenate([gain_ref[core], gain_ref[other]], axis=1)

    def inputs_of(at):
        kind = frames[at]
        frame = kind[1] if kind[0] == "k" else GROUP + kind[2] * RING + kind[1]
        six = jnp.concatenate([ray[frame : frame + 1] for ray in rays] + [zeros], axis=0)
        high, mid, low = split3(six)
        stacked = jnp.concatenate([high, high, mid, mid, high, low], axis=0).astype(BF16)
        embedded = lax.dot_general(stacked, embeds, (((0,), (0,)), ((), ())), preferred_element_type=F32)
        return (block_buf[at].astype(F32) + embedded).astype(BF16)

    def normed(inputs):
        wide = inputs.astype(F32)
        factor = lax.rsqrt(jnp.sum(wide * wide, axis=-1, keepdims=True) * (1.0 / WIDTH) + 1e-06)
        return (wide * factor * gains).astype(BF16)

    def project(rows, which):
        return mm(rows, qkv_ref[which])

    own_ref[...] = cams[0:1]
    at = 0
    for group in list(keys) + list(queries):
        members = range(at, at + len(group))
        for member in members:
            for copy in waits[member]:
                copy.wait()
        raw = [inputs_of(member) for member in members]
        pair = jnp.concatenate([normed(part) for part in raw], axis=0)
        if frames[at][0] == "k":
            if at == 0:
                for copy in weights[1] + weights[2]:
                    copy.wait()
            span = slice(at * ROWS, (at + len(group)) * ROWS)
            k_ref[span, :] = project(pair, 1).astype(BF16)
            v_ref[span, :] = project(pair, 2).astype(BF16)
            rows = pl.ds(at * ROWS, len(group) * ROWS)
            send(k_ref.at[rows], k_hbm.at[rows])
            send(v_ref.at[rows], v_hbm.at[rows])
        else:
            if group is queries[0]:
                for copy in weights[0]:
                    copy.wait()
            query = (project(pair, 0) * (LOG2E / HEAD_DIM**0.5)).astype(BF16)
            for spot, (by_x, by_y) in enumerate(group):
                if (by_x, by_y) == (0, 0):
                    share_ref[...] = raw[spot][:, :HALF]
                held = at + spot - GROUP
                q_ref[held] = query[spot * ROWS : (spot + 1) * ROWS]
                send(q_ref.at[held], q_hbm.at[RING + ((at_x - by_x) & (RING - 1)) if by_y else by_x])
        at += len(group)
    for copy in sent:
        copy.wait()


def prep(keys, queries, cams, more, embed, gain, qkv, blocks):
    any_space = pl.BlockSpec(memory_space=pltpu.HBM)
    spots = []
    for array, value in enumerate(blocks):
        spots += [(array, None)] if value[0].ndim == 2 else [(array, plane) for plane in range(2)]
    count = len(spots)
    blocks = [item for value in blocks for item in value]
    wide = jax.ShapeDtypeStruct((GROUP * ROWS, HALF), BF16)
    shapes = [
        wide,
        wide,
        jax.ShapeDtypeStruct((GROUP, ROWS, HALF), BF16),
        jax.ShapeDtypeStruct((ROWS, HALF), BF16),
        jax.ShapeDtypeStruct((1, CAM), F32),
    ]
    return pl.pallas_call(
        functools.partial(prep_kernel, keys, queries, tuple(spots)),
        in_specs=[VMEM] * 4 + [any_space] * (1 + len(blocks)),
        out_specs=[any_space] * 3 + [VMEM] * 2,
        out_shape=shapes,
        scratch_shapes=[
            pltpu.VMEM((3, WIDTH, HALF), BF16),
            pltpu.VMEM((count, ROWS, WIDTH), BF16),
            pltpu.VMEM((GROUP * ROWS, HALF), BF16),
            pltpu.VMEM((GROUP * ROWS, HALF), BF16),
            pltpu.VMEM((GROUP, ROWS, HALF), BF16),
            pltpu.SemaphoreType.DMA((2 * count + 6,)),
            pltpu.SemaphoreType.DMA((2 * len(keys) + GROUP,)),
        ],
        compiler_params=pltpu.CompilerParams(vmem_limit_bytes=VMEM_LIMIT),
        name="prep",
    )(cams, more, embed, gain, qkv, *blocks)


def pack_levels(out_ref, index, compact):
    out_ref[index, ROWS:TALL, :] = jnp.zeros((TALL - ROWS, HALF), BF16)
    out_ref[index, ROWS:TALL, 0:ROWS] = compact[0:16].astype(BF16)
    out_ref[index, ROWS:TALL, 256 : 256 + ROWS] = compact[16:32].astype(BF16)


def attend_kernel(q_ref, k_ref, v_ref, *out_refs):
    lane = lax.broadcasted_iota(jnp.int32, (1, 128), 1)
    count = q_ref.shape[0]
    places = [(out_refs[0], at) for at in range(count)] if len(out_refs) < count else [(ref, 0) for ref in out_refs]
    ones = jnp.ones((k_ref.shape[0], 128), BF16)
    stat = None
    for pair in range(PAIRS):
        part = slice(pair * 128, pair * 128 + 128)
        query = jnp.concatenate([q_ref[at, :, part] for at in range(count)], axis=0)
        keys = k_ref[:, part]
        values = v_ref[:, part]
        joined = None
        for side in range(2):
            mine = (lane >> 6) == side
            scores = mm_t(jnp.where(mine, query, jnp.zeros_like(query)), keys)
            top = jnp.max(scores, axis=-1, keepdims=True)
            weights = jnp.exp2(scores - top).astype(BF16)
            extended = jnp.concatenate([jnp.where(mine, values, jnp.zeros_like(values)), ones], axis=1)
            both = mm(weights, extended)
            total = both[:, 128:]
            result = both[:, :128] / total
            joined = result if joined is None else joined + result
            level = top + jnp.log2(total)
            head = pair * 2 + side
            stat = level if stat is None else jnp.where((lane & 7) == head, level, stat)
        joined = joined.astype(BF16)
        for at, (ref, index) in enumerate(places):
            ref[index, 0:ROWS, part] = joined[at * ROWS : (at + 1) * ROWS]
    high, mid, low = split3(stat)
    packed = jnp.where(lane < 8, high, jnp.where(lane < 16, mid, jnp.where(lane < 24, low, 0.0))).astype(BF16)
    same = lax.broadcasted_iota(jnp.int32, (32, 128), 0) == lax.broadcasted_iota(jnp.int32, (32, 128), 1)
    pick = jnp.where(same, 1.0, 0.0).astype(BF16)
    for at, (ref, index) in enumerate(places):
        pack_levels(ref, index, mm_t(pick, packed[at * ROWS : (at + 1) * ROWS]))


def attend(query, keys, values, first, count, together):
    shape = (RING, TALL, HALF) if together else (1, TALL, HALF)
    spans = RING // count if together else 1
    outs = 1 if together else count
    block = (count if together else 1, TALL, HALF)
    return pl.pallas_call(
        attend_kernel,
        grid=(spans,),
        in_specs=[
            pl.BlockSpec((pl.Element(count), pl.Element(ROWS), pl.Element(HALF)), lambda i: (first + i * count, 0, 0)),
            VMEM,
            VMEM,
        ],
        out_specs=[pl.BlockSpec(block, lambda i: (i, 0, 0))] * outs,
        out_shape=[jax.ShapeDtypeStruct(shape, BF16)] * outs,
        compiler_params=pltpu.CompilerParams(vmem_limit_bytes=VMEM_LIMIT),
        name="attend",
    )(query, keys, values)


def join_parts(parts):
    row = lax.broadcasted_iota(jnp.int32, (32, HALF), 0)
    column = lax.broadcasted_iota(jnp.int32, (32, HALF), 1)
    spread = jnp.where(((row & 7) == (column >> 6)) & (row < 24), 1.0, 0.0).astype(BF16)
    levels = []
    for ref, index in parts:
        compact = jnp.concatenate(
            [ref[index, ROWS:TALL, 0:ROWS], ref[index, ROWS:TALL, 256 : 256 + ROWS]], axis=0
        )
        levels.append(
            lax.dot_general(compact, spread, (((0,), (0,)), ((), ())), preferred_element_type=F32)
        )
    top = levels[0]
    for level in levels[1:]:
        top = jnp.maximum(top, level)
    total = None
    mixed = None
    for (ref, index), level in zip(parts, levels):
        weight = jnp.exp2(level - top)
        value = weight * ref[index, 0:ROWS, :].astype(F32)
        total = weight if total is None else total + weight
        mixed = value if mixed is None else mixed + value
    return mixed / total, top, total


def join_kernel(parts_ref, out_ref):
    result, top, total = join_parts([(parts_ref, at) for at in range(RING)])
    out_ref[0, 0:ROWS, :] = result.astype(BF16)
    row = lax.broadcasted_iota(jnp.int32, (8, HALF), 0)
    column = lax.broadcasted_iota(jnp.int32, (8, HALF), 1)
    pick = jnp.where(row * HEAD_DIM == column, 1.0, 0.0).astype(BF16)
    pieces = [mm_t(pick, piece.astype(BF16)) for piece in split3(top + jnp.log2(total))]
    pack_levels(out_ref, 0, jnp.concatenate(pieces + [jnp.zeros((8, ROWS), F32)], axis=0))


def join(parts):
    return pl.pallas_call(
        join_kernel,
        out_shape=jax.ShapeDtypeStruct((1, TALL, HALF), BF16),
        compiler_params=pltpu.CompilerParams(vmem_limit_bytes=VMEM_LIMIT),
        name="join",
    )(parts)


def merge_kernel(out_ref, *refs):
    parts, (mine_ref, send_ref) = refs[:-2], refs[-2:]
    core = lax.axis_index("h")
    result, _, _ = join_parts([(ref, 0) for ref in parts])
    attended = result.astype(BF16)
    mine_ref[...] = mm(attended, out_ref[:, pl.ds(pl.multiple_of(core * HALF, HALF), HALF)])
    send_ref[...] = mm(attended, out_ref[:, pl.ds(pl.multiple_of((1 - core) * HALF, HALF), HALF)]).astype(BF16)


def merge(render_out, parts):
    return pl.pallas_call(
        merge_kernel,
        in_specs=[VMEM] * (1 + len(parts)),
        out_specs=[VMEM] * 2,
        out_shape=[
            jax.ShapeDtypeStruct((ROWS, HALF), F32),
            jax.ShapeDtypeStruct((ROWS, HALF), BF16),
        ],
        compiler_params=pltpu.CompilerParams(vmem_limit_bytes=VMEM_LIMIT),
        name="merge",
    )(render_out, *parts)


def shift(value, axis, size, by):
    return lax.ppermute(value, axis, [(at, (at + by) % size) for at in range(size)])


def local(
    tokens,
    frame_order,
    target_mask,
    pose_norm,
    pose_qkv,
    pose_out,
    camera_head,
    ray_embed,
    render_norm,
    render_qkv,
    render_out,
):
    send, near, far = start(frame_order, target_mask, tokens)

    def other(value):
        return shift(value, "h", 2, 1)

    def step_up(value):
        return shift(value, "z", 8, 1)

    def step_down(value):
        return shift(value, "z", 8, 7)

    tie = lax.optimization_barrier
    cam_all = lax.all_to_all(send, ("x", "y", "z"), 0, 0)
    up1, down1, across = step_up(near), step_down(near), shift(near, "y", 2, 1)
    opposite = shift(near, "z", 8, 4)
    cam_all, up1, down1, across = tie((cam_all, up1, down1, across))
    up2, down2 = step_up(up1), step_down(down1)
    planes = jnp.stack([near, across])
    side1, side3, side2 = (shift(planes, "x", 4, by) for by in (1, 3, 2))
    cams = pose(cam_all, pose_norm[None, :], pose_qkv, pose_out, camera_head.T)
    cams, up2, down2, opposite = tie((cams, up2, down2, opposite))
    more = other(cams)
    up3, down3 = step_up(up2), step_down(down2)
    more, up3, down3, side1, side3, side2 = tie((more, up3, down3, side1, side3, side2))
    gain = render_norm.reshape(2, 1, HALF)
    qkv = render_qkv.reshape(3, 2, HALF, HALF)

    def pair(value):
        return (value, other(value))

    own_pair = (near, far)
    key, val, query, share, own = prep(
        ((0, 1, 7, 2), (6, 4, 3, 5)),
        (((0, 0), (0, 1)), ((1, 0), (1, 1), (3, 0), (3, 1)), ((2, 0), (2, 1))),
        cams,
        more,
        ray_embed,
        gain,
        qkv,
        [own_pair]
        + [pair(value) for value in (up1, down1, up2, down2, opposite, up3, down3)]
        + [own_pair]
        + [pair(value) for value in (across, side1, side3, side2)],
    )
    far_parts = lax.all_to_all(attend(query, key, val, RING, 2, True)[0], "x", 0, 0)
    sides = [shift(part, "x", 4, -by) for by, part in zip((1, 2, 3), attend(query, key, val, 1, 3, False))]
    crossed = join(far_parts)
    query, crossed = tie((query, crossed))
    crossed = shift(crossed, "y", 2, 1)
    nearest = attend(query, key, val, 0, 1, False)
    mine, outgoing = merge(render_out, [*nearest, crossed, *sides])
    theirs = other(outgoing)
    rendered = (share.astype(F32) + (mine + theirs.astype(F32))).astype(BF16)
    return (rendered, own)


def solution(mesh):
    fine = Mesh(mesh.devices.reshape(4, 2, 8, 2, 2), ("x", "y", "z", "h", "dp"))
    rows = ("dp", "x", "y", "z")
    in_specs = (
        P(rows, None),
        P(rows),
        P(rows),
        P(),
        P(None, None, "h"),
        P("h", None),
        P(),
        P(),
        P(),
        P(None, None, "h"),
        P("h", None),
    )
    out_specs = (P(rows, "h"), P(rows, None))
    return jax.shard_map(local, mesh=fine, in_specs=in_specs, out_specs=out_specs, check_vma=False)
```

```python
import functools

import jax
import jax.numpy as jnp
from jax import lax
from jax.experimental import pallas as pl
from jax.experimental.pallas import tpu as pltpu
from jax.sharding import Mesh
from jax.sharding import PartitionSpec as P

F32 = jnp.float32
BF16 = jnp.bfloat16
HEAD_DIM = 64
GRID = 32
ROWS = 192
WIDTH = 1024
HALF = 512
HEADS = 8
PAIRS = 4
GROUP = 8
RING = 4
TALL = 208
CAM = 12
FRAMES = 64
LOG2E = 1.4426950408889634
MIB = 1024 * 1024
VMEM_LIMIT = 56 * MIB
SMEM = pl.BlockSpec(memory_space=pltpu.SMEM)
VMEM = pl.BlockSpec(memory_space=pltpu.VMEM)


def split3(value):
    high = value.astype(BF16).astype(F32)
    rest = value - high
    mid = rest.astype(BF16).astype(F32)
    return high, mid, rest - mid


def mm(left, right):
    return jnp.dot(left, right, preferred_element_type=F32)


def mm_t(left, right):
    return lax.dot_general(left, right, (((1,), (1,)), ((), ())), preferred_element_type=F32)


def start_kernel(order_ref, mask_ref, tokens_ref, send_ref, near_ref, far_ref):
    tokens = tokens_ref[...].astype(F32)
    pooled = jnp.sum(tokens, axis=0, keepdims=True) * (1.0 / ROWS)
    pieces = [pooled[:, at * 128 : at * 128 + 128] for at in range(8)]
    index = lax.broadcasted_iota(jnp.int32, (8, 128), 0) * 128 + lax.broadcasted_iota(jnp.int32, (8, 128), 1)
    rate = jnp.exp(-4.0 * index.astype(F32) / WIDTH)
    wave = jnp.sin(order_ref[0].astype(F32) * rate)
    cam = (jnp.concatenate(pieces, axis=0) + wave).astype(BF16).astype(F32)
    send_ref[...] = jnp.broadcast_to(cam[None], send_ref.shape)
    kept = (tokens * (1 - mask_ref[0]).astype(F32)).astype(BF16)
    first = lax.axis_index("h") == 0
    near_ref[...] = jnp.where(first, kept[:, :HALF], kept[:, HALF:])
    far_ref[...] = jnp.where(first, kept[:, HALF:], kept[:, :HALF])


def start(order, mask, tokens):
    return pl.pallas_call(
        start_kernel,
        in_specs=[SMEM, SMEM, VMEM],
        out_specs=[VMEM] * 3,
        out_shape=[
            jax.ShapeDtypeStruct((FRAMES, 8, 128), F32),
            jax.ShapeDtypeStruct((ROWS, HALF), BF16),
            jax.ShapeDtypeStruct((ROWS, HALF), BF16),
        ],
        compiler_params=pltpu.CompilerParams(vmem_limit_bytes=VMEM_LIMIT),
        name="start",
    )(order, mask, tokens)


def pose_kernel(cam_ref, gain_ref, qkv_hbm, out_hbm, head_ref, cams_ref, qkv_ref, out_ref, sems):
    copies = [pltpu.make_async_copy(qkv_hbm.at[at], qkv_ref.at[at], sems.at[at]) for at in range(3)]
    copies.append(pltpu.make_async_copy(out_hbm, out_ref, sems.at[3]))
    for copy in copies:
        copy.start()
    cam = jnp.concatenate([cam_ref[:, at, :] for at in range(8)], axis=1)
    mean = jnp.mean(cam * cam, axis=-1, keepdims=True)
    normed = (cam * lax.rsqrt(mean + 1e-06) * gain_ref[...]).astype(BF16)
    copies[0].wait()
    query = mm(normed, qkv_ref[0]).astype(BF16)
    copies[1].wait()
    keys = mm(normed, qkv_ref[1]).astype(BF16)
    copies[2].wait()
    values = mm(normed, qkv_ref[2]).astype(BF16)
    lane_head = lax.broadcasted_iota(jnp.int32, (FRAMES, HALF), 1) >> 6
    stacked = jnp.concatenate(
        [jnp.where(lane_head == head, query, jnp.zeros_like(query)) for head in range(HEADS)], axis=0
    )
    scores = mm_t(stacked, keys) * (1.0 / HEAD_DIM**0.5)
    weights = jnp.exp(scores - jnp.max(scores, axis=-1, keepdims=True))
    total = jnp.sum(weights, axis=-1, keepdims=True)
    mixed = mm(weights.astype(BF16), values) / total
    picked = None
    for head in range(HEADS):
        rows = mixed[head * FRAMES : (head + 1) * FRAMES]
        picked = rows if picked is None else jnp.where(lane_head == head, rows, picked)
    copies[3].wait()
    partial = mm(picked.astype(BF16), out_ref[...]) + 0.5 * cam
    cams_ref[...] = lax.dot_general(
        partial,
        head_ref[...],
        (((1,), (1,)), ((), ())),
        precision=lax.Precision.HIGHEST,
        preferred_element_type=F32,
    )


def pose(cam_all, pose_norm, pose_qkv, pose_out, camera_head):
    return pl.pallas_call(
        pose_kernel,
        in_specs=[VMEM, VMEM] + [pl.BlockSpec(memory_space=pltpu.HBM)] * 2 + [VMEM],
        scratch_shapes=[
            pltpu.VMEM((3, WIDTH, HALF), BF16),
            pltpu.VMEM((HALF, WIDTH), BF16),
            pltpu.SemaphoreType.DMA((4,)),
        ],
        out_shape=jax.ShapeDtypeStruct((FRAMES, CAM), F32),
        compiler_params=pltpu.CompilerParams(vmem_limit_bytes=VMEM_LIMIT),
        name="pose",
    )(cam_all, pose_norm, pose_qkv, pose_out, camera_head)


def ray_rows(cams):
    frames = cams.shape[0]
    place_at = lax.broadcasted_iota(jnp.int32, (frames, ROWS), 1)
    across = ((place_at & (GRID - 1)).astype(F32) + 0.5) * (2.0 / GRID) - 1.0
    down = ((place_at >> 5).astype(F32) + 0.5) * (2.0 / GRID) - 1.0
    squashed = jnp.tanh(cams)

    def turn(which):
        return squashed[:, which : which + 1] * 0.3

    def place(which):
        return squashed[:, 9 + which : 10 + which] * 2.0

    one = (1.0 + turn(0)) * across + turn(1) * down + turn(2)
    two = turn(3) * across + (1.0 + turn(4)) * down + turn(5)
    three = turn(6) * across + turn(7) * down + (1.0 + turn(8))
    length = jnp.sqrt(one * one + two * two + three * three)
    u_one, u_two, u_three = one / length, two / length, three / length
    return (
        u_one,
        u_two,
        u_three,
        place(1) * u_three - place(2) * u_two,
        place(2) * u_one - place(0) * u_three,
        place(0) * u_two - place(1) * u_one,
    )


def prep_kernel(keys, queries, spots, cams_ref, more_ref, embed_ref, gain_ref, qkv_hbm, *refs):
    frames = [("k", offset) for group in keys for offset in group] + [("q",) + spot for group in queries for spot in group]
    arrays = 2 * (max(spot[0] for spot in spots) + 1)
    inputs = refs[:arrays]
    k_hbm, v_hbm, q_hbm, share_ref, own_ref = refs[arrays : arrays + 5]
    qkv_ref, block_buf, k_ref, v_ref, q_ref, sems, out_sems = refs[arrays + 5 :]
    sent = []

    def send(source, target):
        copy = pltpu.make_async_copy(source, target, out_sems.at[len(sent)])
        copy.start()
        sent.append(copy)

    at_x, at_y, at_z, core = (lax.axis_index(name) for name in ("x", "y", "z", "h"))
    other = 1 - core
    copies = []

    def fetch(source, target):
        copy = pltpu.make_async_copy(source, target, sems.at[len(copies)])
        copy.start()
        copies.append(copy)
        return copy

    groups = list(keys) + list(queries)
    firsts = [sum(len(group) for group in groups[:index]) for index in range(len(groups))]
    waits = {}

    def fetch_group(index):
        for at in range(firsts[index], firsts[index] + len(groups[index])):
            array, plane = spots[at]
            pair = inputs[2 * array : 2 * array + 2]
            if plane is not None:
                pair = [ref.at[plane] for ref in pair]
            waits[at] = [
                fetch(ref, block_buf.at[at, :, pl.ds(side * HALF, HALF)]) for side, ref in enumerate(pair)
            ]

    fetch_group(0)
    weights = {
        which: [
            fetch(qkv_hbm.at[which, side], qkv_ref.at[which, pl.ds(at * HALF, HALF)])
            for at, side in enumerate((core, other))
        ]
        for which in (1, 2, 0)
    }
    fetch_group(1)
    row = lax.broadcasted_iota(jnp.int32, (2 * GROUP, FRAMES), 0)
    key_frame = at_x * 16 + at_y * 8 + ((at_z - row) & 7)
    query_frame = ((at_x - row) & 3) * 16 + ((at_y - (row >> 2)) & 1) * 8 + at_z
    wanted = jnp.where(row < GROUP, key_frame, query_frame)
    pick = jnp.where(lax.broadcasted_iota(jnp.int32, (2 * GROUP, FRAMES), 1) == wanted, 1.0, 0.0)
    cams = jnp.dot(
        pick, cams_ref[...] + more_ref[...], precision=lax.Precision.HIGHEST, preferred_element_type=F32
    )
    rays = ray_rows(cams)
    zeros = jnp.zeros((2, ROWS), F32)
    embeds = []
    for side in (core, other):
        pad = jnp.zeros((2, HALF), F32)
        span = pl.ds(pl.multiple_of(side * HALF, HALF), HALF)
        high, mid, low = split3(jnp.concatenate([embed_ref[:, span], pad], axis=0))
        embeds.append(jnp.concatenate([high, mid, high, mid, low, high], axis=0).astype(BF16))
    embeds = jnp.concatenate(embeds, axis=1)
    gains = jnp.concatenate([gain_ref[core], gain_ref[other]], axis=1)

    def inputs_of(at):
        kind = frames[at]
        frame = kind[1] if kind[0] == "k" else GROUP + kind[2] * RING + kind[1]
        six = jnp.concatenate([ray[frame : frame + 1] for ray in rays] + [zeros], axis=0)
        high, mid, low = split3(six)
        stacked = jnp.concatenate([high, high, mid, mid, high, low], axis=0).astype(BF16)
        embedded = lax.dot_general(stacked, embeds, (((0,), (0,)), ((), ())), preferred_element_type=F32)
        return (block_buf[at].astype(F32) + embedded).astype(BF16)

    def normed(inputs):
        wide = inputs.astype(F32)
        factor = lax.rsqrt(jnp.sum(wide * wide, axis=-1, keepdims=True) * (1.0 / WIDTH) + 1e-06)
        return (wide * factor * gains).astype(BF16)

    def project(rows, which):
        return mm(rows, qkv_ref[which])

    own_ref[...] = cams[0:1]
    for index, group in enumerate(groups):
        at = firsts[index]
        members = range(at, at + len(group))
        if index + 2 < len(groups):
            fetch_group(index + 2)
        for member in members:
            for copy in waits[member]:
                copy.wait()
        raw = [inputs_of(member) for member in members]
        pair = jnp.concatenate([normed(part) for part in raw], axis=0)
        if frames[at][0] == "k":
            if at == 0:
                for copy in weights[1] + weights[2]:
                    copy.wait()
            span = slice(at * ROWS, (at + len(group)) * ROWS)
            k_ref[span, :] = project(pair, 1).astype(BF16)
            v_ref[span, :] = project(pair, 2).astype(BF16)
            rows = pl.ds(at * ROWS, len(group) * ROWS)
            send(k_ref.at[rows], k_hbm.at[rows])
            send(v_ref.at[rows], v_hbm.at[rows])
        else:
            if group is queries[0]:
                for copy in weights[0]:
                    copy.wait()
            query = (project(pair, 0) * (LOG2E / HEAD_DIM**0.5)).astype(BF16)
            for spot, (by_x, by_y) in enumerate(group):
                if (by_x, by_y) == (0, 0):
                    share_ref[...] = raw[spot][:, :HALF]
                held = at + spot - GROUP
                q_ref[held] = query[spot * ROWS : (spot + 1) * ROWS]
                send(q_ref.at[held], q_hbm.at[RING + ((at_x - by_x) & (RING - 1)) if by_y else by_x])
    for copy in sent:
        copy.wait()


def prep(keys, queries, cams, more, embed, gain, qkv, blocks):
    any_space = pl.BlockSpec(memory_space=pltpu.HBM)
    spots = []
    for array, value in enumerate(blocks):
        spots += [(array, None)] if value[0].ndim == 2 else [(array, plane) for plane in range(2)]
    count = len(spots)
    blocks = [item for value in blocks for item in value]
    wide = jax.ShapeDtypeStruct((GROUP * ROWS, HALF), BF16)
    shapes = [
        wide,
        wide,
        jax.ShapeDtypeStruct((GROUP, ROWS, HALF), BF16),
        jax.ShapeDtypeStruct((ROWS, HALF), BF16),
        jax.ShapeDtypeStruct((1, CAM), F32),
    ]
    return pl.pallas_call(
        functools.partial(prep_kernel, keys, queries, tuple(spots)),
        in_specs=[VMEM] * 4 + [any_space] * (1 + len(blocks)),
        out_specs=[any_space] * 3 + [VMEM] * 2,
        out_shape=shapes,
        scratch_shapes=[
            pltpu.VMEM((3, WIDTH, HALF), BF16),
            pltpu.VMEM((count, ROWS, WIDTH), BF16),
            pltpu.VMEM((GROUP * ROWS, HALF), BF16),
            pltpu.VMEM((GROUP * ROWS, HALF), BF16),
            pltpu.VMEM((GROUP, ROWS, HALF), BF16),
            pltpu.SemaphoreType.DMA((2 * count + 6,)),
            pltpu.SemaphoreType.DMA((2 * len(keys) + GROUP,)),
        ],
        compiler_params=pltpu.CompilerParams(vmem_limit_bytes=VMEM_LIMIT),
        name="prep",
    )(cams, more, embed, gain, qkv, *blocks)


def pack_levels(out_ref, index, compact):
    out_ref[index, ROWS:TALL, :] = jnp.zeros((TALL - ROWS, HALF), BF16)
    out_ref[index, ROWS:TALL, 0:ROWS] = compact[0:16].astype(BF16)
    out_ref[index, ROWS:TALL, 256 : 256 + ROWS] = compact[16:32].astype(BF16)


def attend_kernel(q_ref, k_ref, v_ref, *out_refs):
    lane = lax.broadcasted_iota(jnp.int32, (1, 128), 1)
    count = q_ref.shape[0]
    places = [(out_refs[0], at) for at in range(count)] if len(out_refs) < count else [(ref, 0) for ref in out_refs]
    ones = jnp.ones((k_ref.shape[0], 128), BF16)
    stat = None
    for pair in range(PAIRS):
        part = slice(pair * 128, pair * 128 + 128)
        query = jnp.concatenate([q_ref[at, :, part] for at in range(count)], axis=0)
        keys = k_ref[:, part]
        values = v_ref[:, part]
        joined = None
        for side in range(2):
            mine = (lane >> 6) == side
            scores = mm_t(jnp.where(mine, query, jnp.zeros_like(query)), keys)
            top = jnp.max(scores, axis=-1, keepdims=True)
            weights = jnp.exp2(scores - top).astype(BF16)
            extended = jnp.concatenate([jnp.where(mine, values, jnp.zeros_like(values)), ones], axis=1)
            both = mm(weights, extended)
            total = both[:, 128:]
            result = both[:, :128] / total
            joined = result if joined is None else joined + result
            level = top + jnp.log2(total)
            head = pair * 2 + side
            stat = level if stat is None else jnp.where((lane & 7) == head, level, stat)
        joined = joined.astype(BF16)
        for at, (ref, index) in enumerate(places):
            ref[index, 0:ROWS, part] = joined[at * ROWS : (at + 1) * ROWS]
    high, mid, low = split3(stat)
    packed = jnp.where(lane < 8, high, jnp.where(lane < 16, mid, jnp.where(lane < 24, low, 0.0))).astype(BF16)
    same = lax.broadcasted_iota(jnp.int32, (32, 128), 0) == lax.broadcasted_iota(jnp.int32, (32, 128), 1)
    pick = jnp.where(same, 1.0, 0.0).astype(BF16)
    for at, (ref, index) in enumerate(places):
        pack_levels(ref, index, mm_t(pick, packed[at * ROWS : (at + 1) * ROWS]))


def attend(query, keys, values, first, count, together):
    shape = (RING, TALL, HALF) if together else (1, TALL, HALF)
    spans = RING // count if together else 1
    outs = 1 if together else count
    block = (count if together else 1, TALL, HALF)
    return pl.pallas_call(
        attend_kernel,
        grid=(spans,),
        in_specs=[
            pl.BlockSpec((pl.Element(count), pl.Element(ROWS), pl.Element(HALF)), lambda i: (first + i * count, 0, 0)),
            VMEM,
            VMEM,
        ],
        out_specs=[pl.BlockSpec(block, lambda i: (i, 0, 0))] * outs,
        out_shape=[jax.ShapeDtypeStruct(shape, BF16)] * outs,
        compiler_params=pltpu.CompilerParams(vmem_limit_bytes=VMEM_LIMIT),
        name="attend",
    )(query, keys, values)


def join_parts(parts):
    row = lax.broadcasted_iota(jnp.int32, (32, HALF), 0)
    column = lax.broadcasted_iota(jnp.int32, (32, HALF), 1)
    spread = jnp.where(((row & 7) == (column >> 6)) & (row < 24), 1.0, 0.0).astype(BF16)
    levels = []
    for ref, index in parts:
        compact = jnp.concatenate(
            [ref[index, ROWS:TALL, 0:ROWS], ref[index, ROWS:TALL, 256 : 256 + ROWS]], axis=0
        )
        levels.append(
            lax.dot_general(compact, spread, (((0,), (0,)), ((), ())), preferred_element_type=F32)
        )
    top = levels[0]
    for level in levels[1:]:
        top = jnp.maximum(top, level)
    total = None
    mixed = None
    for (ref, index), level in zip(parts, levels):
        weight = jnp.exp2(level - top)
        value = weight * ref[index, 0:ROWS, :].astype(F32)
        total = weight if total is None else total + weight
        mixed = value if mixed is None else mixed + value
    return mixed / total, top, total


def join_kernel(parts_ref, out_ref):
    result, top, total = join_parts([(parts_ref, at) for at in range(RING)])
    out_ref[0, 0:ROWS, :] = result.astype(BF16)
    row = lax.broadcasted_iota(jnp.int32, (8, HALF), 0)
    column = lax.broadcasted_iota(jnp.int32, (8, HALF), 1)
    pick = jnp.where(row * HEAD_DIM == column, 1.0, 0.0).astype(BF16)
    pieces = [mm_t(pick, piece.astype(BF16)) for piece in split3(top + jnp.log2(total))]
    pack_levels(out_ref, 0, jnp.concatenate(pieces + [jnp.zeros((8, ROWS), F32)], axis=0))


def join(parts):
    return pl.pallas_call(
        join_kernel,
        out_shape=jax.ShapeDtypeStruct((1, TALL, HALF), BF16),
        compiler_params=pltpu.CompilerParams(vmem_limit_bytes=8 * MIB),
        name="join",
    )(parts)


def merge_kernel(out_ref, *refs):
    parts, (mine_ref, send_ref) = refs[:-2], refs[-2:]
    core = lax.axis_index("h")
    result, _, _ = join_parts([(ref, 0) for ref in parts])
    attended = result.astype(BF16)
    mine_ref[...] = mm(attended, out_ref[:, pl.ds(pl.multiple_of(core * HALF, HALF), HALF)])
    send_ref[...] = mm(attended, out_ref[:, pl.ds(pl.multiple_of((1 - core) * HALF, HALF), HALF)]).astype(BF16)


def merge(render_out, parts):
    return pl.pallas_call(
        merge_kernel,
        in_specs=[VMEM] * (1 + len(parts)),
        out_specs=[VMEM] * 2,
        out_shape=[
            jax.ShapeDtypeStruct((ROWS, HALF), F32),
            jax.ShapeDtypeStruct((ROWS, HALF), BF16),
        ],
        compiler_params=pltpu.CompilerParams(vmem_limit_bytes=10 * MIB),
        name="merge",
    )(render_out, *parts)


def shift(value, axis, size, by):
    return lax.ppermute(value, axis, [(at, (at + by) % size) for at in range(size)])


def local(
    tokens,
    frame_order,
    target_mask,
    pose_norm,
    pose_qkv,
    pose_out,
    camera_head,
    ray_embed,
    render_norm,
    render_qkv,
    render_out,
):
    send, near, far = start(frame_order, target_mask, tokens)

    def other(value):
        return shift(value, "h", 2, 1)

    def step_up(value):
        return shift(value, "z", 8, 1)

    def step_down(value):
        return shift(value, "z", 8, 7)

    tie = lax.optimization_barrier
    cam_all = lax.all_to_all(send, ("x", "y", "z"), 0, 0)
    up1, down1, across = step_up(near), step_down(near), shift(near, "y", 2, 1)
    opposite = shift(near, "z", 8, 4)
    cam_all, up1, down1, across = tie((cam_all, up1, down1, across))
    up2, down2 = step_up(up1), step_down(down1)
    planes = jnp.stack([near, across])
    side1, side3, side2 = (shift(planes, "x", 4, by) for by in (1, 3, 2))
    cams = pose(cam_all, pose_norm[None, :], pose_qkv, pose_out, camera_head.T)
    cams, up2, down2, opposite = tie((cams, up2, down2, opposite))
    more = other(cams)
    up3, down3 = step_up(up2), step_down(down2)
    more, up3, down3, side1, side3, side2 = tie((more, up3, down3, side1, side3, side2))
    gain = render_norm.reshape(2, 1, HALF)
    qkv = render_qkv.reshape(3, 2, HALF, HALF)

    def pair(value):
        return (value, other(value))

    own_pair = (near, far)
    key, val, query, share, own = prep(
        ((0, 1, 7, 2), (6, 4, 3, 5)),
        (((0, 0), (0, 1)), ((1, 0), (1, 1), (3, 0), (3, 1)), ((2, 0), (2, 1))),
        cams,
        more,
        ray_embed,
        gain,
        qkv,
        [own_pair]
        + [pair(value) for value in (up1, down1, up2, down2, opposite, up3, down3)]
        + [own_pair]
        + [pair(value) for value in (across, side1, side3, side2)],
    )
    far_parts = lax.all_to_all(attend(query, key, val, RING, 2, True)[0], "x", 0, 0)
    sides = [shift(part, "x", 4, -by) for by, part in zip((1, 2, 3), attend(query, key, val, 1, 3, False))]
    crossed = join(far_parts)
    query, crossed = tie((query, crossed))
    crossed = shift(crossed, "y", 2, 1)
    nearest = attend(query, key, val, 0, 1, False)
    mine, outgoing = merge(render_out, [*nearest, crossed, *sides])
    theirs = other(outgoing)
    rendered = (share.astype(F32) + (mine + theirs.astype(F32))).astype(BF16)
    return (rendered, own)


def solution(mesh):
    fine = Mesh(mesh.devices.reshape(4, 2, 8, 2, 2), ("x", "y", "z", "h", "dp"))
    rows = ("dp", "x", "y", "z")
    in_specs = (
        P(rows, None),
        P(rows),
        P(rows),
        P(),
        P(None, None, "h"),
        P("h", None),
        P(),
        P(),
        P(),
        P(None, None, "h"),
        P("h", None),
    )
    out_specs = (P(rows, "h"), P(rows, None))
    return jax.shard_map(local, mesh=fine, in_specs=in_specs, out_specs=out_specs, check_vma=False)
```

```python
import functools

import jax
import jax.numpy as jnp
from jax import lax
from jax.experimental import pallas as pl
from jax.experimental.pallas import tpu as pltpu
from jax.sharding import Mesh
from jax.sharding import PartitionSpec as P

F32 = jnp.float32
BF16 = jnp.bfloat16
HEAD_DIM = 64
GRID = 32
ROWS = 192
WIDTH = 1024
HALF = 512
HEADS = 8
PAIRS = 4
GROUP = 8
RING = 4
TALL = 208
CAM = 12
FRAMES = 64
LOG2E = 1.4426950408889634
MIB = 1024 * 1024
VMEM_LIMIT = 56 * MIB
SMEM = pl.BlockSpec(memory_space=pltpu.SMEM)
VMEM = pl.BlockSpec(memory_space=pltpu.VMEM)


def split3(value):
    high = value.astype(BF16).astype(F32)
    rest = value - high
    mid = rest.astype(BF16).astype(F32)
    return high, mid, rest - mid


def mm(left, right):
    return jnp.dot(left, right, preferred_element_type=F32)


def mm_t(left, right):
    return lax.dot_general(left, right, (((1,), (1,)), ((), ())), preferred_element_type=F32)


def start_kernel(order_ref, mask_ref, tokens_ref, send_ref, near_ref, far_ref):
    tokens = tokens_ref[...].astype(F32)
    pooled = jnp.sum(tokens, axis=0, keepdims=True) * (1.0 / ROWS)
    pieces = [pooled[:, at * 128 : at * 128 + 128] for at in range(8)]
    index = lax.broadcasted_iota(jnp.int32, (8, 128), 0) * 128 + lax.broadcasted_iota(jnp.int32, (8, 128), 1)
    rate = jnp.exp(-4.0 * index.astype(F32) / WIDTH)
    wave = jnp.sin(order_ref[0].astype(F32) * rate)
    cam = (jnp.concatenate(pieces, axis=0) + wave).astype(BF16).astype(F32)
    send_ref[...] = jnp.broadcast_to(cam[None], send_ref.shape)
    kept = (tokens * (1 - mask_ref[0]).astype(F32)).astype(BF16)
    first = lax.axis_index("h") == 0
    near_ref[...] = jnp.where(first, kept[:, :HALF], kept[:, HALF:])
    far_ref[...] = jnp.where(first, kept[:, HALF:], kept[:, :HALF])


def start(order, mask, tokens):
    return pl.pallas_call(
        start_kernel,
        in_specs=[SMEM, SMEM, VMEM],
        out_specs=[VMEM] * 3,
        out_shape=[
            jax.ShapeDtypeStruct((FRAMES, 8, 128), F32),
            jax.ShapeDtypeStruct((ROWS, HALF), BF16),
            jax.ShapeDtypeStruct((ROWS, HALF), BF16),
        ],
        compiler_params=pltpu.CompilerParams(vmem_limit_bytes=VMEM_LIMIT),
        name="start",
    )(order, mask, tokens)


def pose_kernel(cam_ref, gain_ref, qkv_hbm, out_hbm, head_ref, cams_ref, qkv_ref, out_ref, sems):
    copies = [pltpu.make_async_copy(qkv_hbm.at[at], qkv_ref.at[at], sems.at[at]) for at in range(3)]
    copies.append(pltpu.make_async_copy(out_hbm, out_ref, sems.at[3]))
    for copy in copies:
        copy.start()
    cam = jnp.concatenate([cam_ref[:, at, :] for at in range(8)], axis=1)
    mean = jnp.mean(cam * cam, axis=-1, keepdims=True)
    normed = (cam * lax.rsqrt(mean + 1e-06) * gain_ref[...]).astype(BF16)
    copies[0].wait()
    query = mm(normed, qkv_ref[0]).astype(BF16)
    copies[1].wait()
    keys = mm(normed, qkv_ref[1]).astype(BF16)
    copies[2].wait()
    values = mm(normed, qkv_ref[2]).astype(BF16)
    lane_head = lax.broadcasted_iota(jnp.int32, (FRAMES, HALF), 1) >> 6
    stacked = jnp.concatenate(
        [jnp.where(lane_head == head, query, jnp.zeros_like(query)) for head in range(HEADS)], axis=0
    )
    scores = mm_t(stacked, keys) * (1.0 / HEAD_DIM**0.5)
    weights = jnp.exp(scores - jnp.max(scores, axis=-1, keepdims=True))
    total = jnp.sum(weights, axis=-1, keepdims=True)
    mixed = mm(weights.astype(BF16), values) / total
    picked = None
    for head in range(HEADS):
        rows = mixed[head * FRAMES : (head + 1) * FRAMES]
        picked = rows if picked is None else jnp.where(lane_head == head, rows, picked)
    copies[3].wait()
    partial = mm(picked.astype(BF16), out_ref[...]) + 0.5 * cam
    cams_ref[...] = lax.dot_general(
        partial,
        head_ref[...],
        (((1,), (1,)), ((), ())),
        precision=lax.Precision.HIGHEST,
        preferred_element_type=F32,
    )


def pose(cam_all, pose_norm, pose_qkv, pose_out, camera_head):
    return pl.pallas_call(
        pose_kernel,
        in_specs=[VMEM, VMEM] + [pl.BlockSpec(memory_space=pltpu.HBM)] * 2 + [VMEM],
        scratch_shapes=[
            pltpu.VMEM((3, WIDTH, HALF), BF16),
            pltpu.VMEM((HALF, WIDTH), BF16),
            pltpu.SemaphoreType.DMA((4,)),
        ],
        out_shape=jax.ShapeDtypeStruct((FRAMES, CAM), F32),
        compiler_params=pltpu.CompilerParams(vmem_limit_bytes=VMEM_LIMIT),
        name="pose",
    )(cam_all, pose_norm, pose_qkv, pose_out, camera_head)


def ray_rows(cams):
    frames = cams.shape[0]
    place_at = lax.broadcasted_iota(jnp.int32, (frames, ROWS), 1)
    across = ((place_at & (GRID - 1)).astype(F32) + 0.5) * (2.0 / GRID) - 1.0
    down = ((place_at >> 5).astype(F32) + 0.5) * (2.0 / GRID) - 1.0
    squashed = jnp.tanh(cams)

    def turn(which):
        return squashed[:, which : which + 1] * 0.3

    def place(which):
        return squashed[:, 9 + which : 10 + which] * 2.0

    one = (1.0 + turn(0)) * across + turn(1) * down + turn(2)
    two = turn(3) * across + (1.0 + turn(4)) * down + turn(5)
    three = turn(6) * across + turn(7) * down + (1.0 + turn(8))
    length = jnp.sqrt(one * one + two * two + three * three)
    u_one, u_two, u_three = one / length, two / length, three / length
    return (
        u_one,
        u_two,
        u_three,
        place(1) * u_three - place(2) * u_two,
        place(2) * u_one - place(0) * u_three,
        place(0) * u_two - place(1) * u_one,
    )


def prep_kernel(keys, queries, spots, cams_ref, more_ref, embed_ref, gain_ref, qkv_hbm, *refs):
    frames = [("k", offset) for group in keys for offset in group] + [("q",) + spot for group in queries for spot in group]
    arrays = 2 * (max(spot[0] for spot in spots) + 1)
    inputs = refs[:arrays]
    k_hbm, v_hbm, q_hbm, share_ref, own_ref = refs[arrays : arrays + 5]
    qkv_ref, block_buf, k_ref, v_ref, q_ref, sems, out_sems = refs[arrays + 5 :]
    sent = []

    def send(source, target):
        copy = pltpu.make_async_copy(source, target, out_sems.at[len(sent)])
        copy.start()
        sent.append(copy)

    at_x, at_y, at_z, core = (lax.axis_index(name) for name in ("x", "y", "z", "h"))
    other = 1 - core
    copies = []

    def fetch(source, target):
        copy = pltpu.make_async_copy(source, target, sems.at[len(copies)])
        copy.start()
        copies.append(copy)
        return copy

    groups = list(keys) + list(queries)
    firsts = [sum(len(group) for group in groups[:index]) for index in range(len(groups))]
    waits = {}

    def fetch_group(index):
        for at in range(firsts[index], firsts[index] + len(groups[index])):
            array, plane = spots[at]
            pair = inputs[2 * array : 2 * array + 2]
            if plane is not None:
                pair = [ref.at[plane] for ref in pair]
            waits[at] = [
                fetch(ref, block_buf.at[at, :, pl.ds(side * HALF, HALF)]) for side, ref in enumerate(pair)
            ]

    fetch_group(0)
    weights = {
        which: [
            fetch(qkv_hbm.at[which, side], qkv_ref.at[which, pl.ds(at * HALF, HALF)])
            for at, side in enumerate((core, other))
        ]
        for which in (1, 2, 0)
    }
    fetch_group(1)
    row = lax.broadcasted_iota(jnp.int32, (2 * GROUP, FRAMES), 0)
    key_frame = at_x * 16 + at_y * 8 + ((at_z - row) & 7)
    query_frame = ((at_x - row) & 3) * 16 + ((at_y - (row >> 2)) & 1) * 8 + at_z
    wanted = jnp.where(row < GROUP, key_frame, query_frame)
    pick = jnp.where(lax.broadcasted_iota(jnp.int32, (2 * GROUP, FRAMES), 1) == wanted, 1.0, 0.0)
    cams = jnp.dot(
        pick, cams_ref[...] + more_ref[...], precision=lax.Precision.HIGHEST, preferred_element_type=F32
    )
    rays = ray_rows(cams)
    zeros = jnp.zeros((2, ROWS), F32)
    embeds = []
    for side in (core, other):
        pad = jnp.zeros((2, HALF), F32)
        span = pl.ds(pl.multiple_of(side * HALF, HALF), HALF)
        high, mid, low = split3(jnp.concatenate([embed_ref[:, span], pad], axis=0))
        embeds.append(jnp.concatenate([high, mid, high, mid, low, high], axis=0).astype(BF16))
    embeds = jnp.concatenate(embeds, axis=1)
    gains = jnp.concatenate([gain_ref[core], gain_ref[other]], axis=1)

    def inputs_of(at):
        kind = frames[at]
        frame = kind[1] if kind[0] == "k" else GROUP + kind[2] * RING + kind[1]
        six = jnp.concatenate([ray[frame : frame + 1] for ray in rays] + [zeros], axis=0)
        high, mid, low = split3(six)
        stacked = jnp.concatenate([high, high, mid, mid, high, low], axis=0).astype(BF16)
        embedded = lax.dot_general(stacked, embeds, (((0,), (0,)), ((), ())), preferred_element_type=F32)
        return (block_buf[at].astype(F32) + embedded).astype(BF16)

    def normed(inputs):
        wide = inputs.astype(F32)
        factor = lax.rsqrt(jnp.sum(wide * wide, axis=-1, keepdims=True) * (1.0 / WIDTH) + 1e-06)
        return (wide * factor * gains).astype(BF16)

    def project(rows, which):
        return mm(rows, qkv_ref[which])

    own_ref[...] = cams[0:1]
    for index, group in enumerate(groups):
        at = firsts[index]
        members = range(at, at + len(group))
        if index + 2 < len(groups):
            fetch_group(index + 2)
        for member in members:
            for copy in waits[member]:
                copy.wait()
        raw = [inputs_of(member) for member in members]
        pair = jnp.concatenate([normed(part) for part in raw], axis=0)
        if frames[at][0] == "k":
            if at == 0:
                for copy in weights[1] + weights[2]:
                    copy.wait()
            span = slice(at * ROWS, (at + len(group)) * ROWS)
            k_ref[span, :] = project(pair, 1).astype(BF16)
            v_ref[span, :] = project(pair, 2).astype(BF16)
            rows = pl.ds(at * ROWS, len(group) * ROWS)
            send(k_ref.at[rows], k_hbm.at[rows])
            send(v_ref.at[rows], v_hbm.at[rows])
        else:
            if group is queries[0]:
                for copy in weights[0]:
                    copy.wait()
            query = (project(pair, 0) * (LOG2E / HEAD_DIM**0.5)).astype(BF16)
            for spot, (by_x, by_y) in enumerate(group):
                if (by_x, by_y) == (0, 0):
                    share_ref[...] = raw[spot][:, :HALF]
                held = at + spot - GROUP
                q_ref[held] = query[spot * ROWS : (spot + 1) * ROWS]
                send(q_ref.at[held], q_hbm.at[RING + ((at_x - by_x) & (RING - 1)) if by_y else by_x])
    for copy in sent:
        copy.wait()


def prep(keys, queries, cams, more, embed, gain, qkv, blocks):
    any_space = pl.BlockSpec(memory_space=pltpu.HBM)
    spots = []
    for array, value in enumerate(blocks):
        spots += [(array, None)] if value[0].ndim == 2 else [(array, plane) for plane in range(2)]
    count = len(spots)
    blocks = [item for value in blocks for item in value]
    wide = jax.ShapeDtypeStruct((GROUP * ROWS, HALF), BF16)
    shapes = [
        wide,
        wide,
        jax.ShapeDtypeStruct((GROUP, ROWS, HALF), BF16),
        jax.ShapeDtypeStruct((ROWS, HALF), BF16),
        jax.ShapeDtypeStruct((1, CAM), F32),
    ]
    return pl.pallas_call(
        functools.partial(prep_kernel, keys, queries, tuple(spots)),
        in_specs=[VMEM] * 4 + [any_space] * (1 + len(blocks)),
        out_specs=[any_space] * 3 + [VMEM] * 2,
        out_shape=shapes,
        scratch_shapes=[
            pltpu.VMEM((3, WIDTH, HALF), BF16),
            pltpu.VMEM((count, ROWS, WIDTH), BF16),
            pltpu.VMEM((GROUP * ROWS, HALF), BF16),
            pltpu.VMEM((GROUP * ROWS, HALF), BF16),
            pltpu.VMEM((GROUP, ROWS, HALF), BF16),
            pltpu.SemaphoreType.DMA((2 * count + 6,)),
            pltpu.SemaphoreType.DMA((2 * len(keys) + GROUP,)),
        ],
        compiler_params=pltpu.CompilerParams(vmem_limit_bytes=VMEM_LIMIT),
        name="prep",
    )(cams, more, embed, gain, qkv, *blocks)


def pack_levels(out_ref, index, compact):
    out_ref[index, ROWS:TALL, :] = jnp.zeros((TALL - ROWS, HALF), BF16)
    out_ref[index, ROWS:TALL, 0:ROWS] = compact[0:16].astype(BF16)
    out_ref[index, ROWS:TALL, 256 : 256 + ROWS] = compact[16:32].astype(BF16)


def attend_kernel(q_ref, k_ref, v_ref, *out_refs):
    lane = lax.broadcasted_iota(jnp.int32, (1, 128), 1)
    count = q_ref.shape[0]
    places = [(out_refs[0], at) for at in range(count)] if len(out_refs) < count else [(ref, 0) for ref in out_refs]
    ones = jnp.ones((k_ref.shape[0], 128), BF16)
    stat = None
    for pair in range(PAIRS):
        part = slice(pair * 128, pair * 128 + 128)
        query = jnp.concatenate([q_ref[at, :, part] for at in range(count)], axis=0)
        keys = k_ref[:, part]
        values = v_ref[:, part]
        joined = None
        for side in range(2):
            mine = (lane >> 6) == side
            scores = mm_t(jnp.where(mine, query, jnp.zeros_like(query)), keys)
            top = jnp.max(scores, axis=-1, keepdims=True)
            weights = jnp.exp2(scores - top).astype(BF16)
            extended = jnp.concatenate([jnp.where(mine, values, jnp.zeros_like(values)), ones], axis=1)
            both = mm(weights, extended)
            total = both[:, 128:]
            result = both[:, :128] / total
            joined = result if joined is None else joined + result
            level = top + jnp.log2(total)
            head = pair * 2 + side
            stat = level if stat is None else jnp.where((lane & 7) == head, level, stat)
        joined = joined.astype(BF16)
        for at, (ref, index) in enumerate(places):
            ref[index, 0:ROWS, part] = joined[at * ROWS : (at + 1) * ROWS]
    high, mid, low = split3(stat)
    packed = jnp.where(lane < 8, high, jnp.where(lane < 16, mid, jnp.where(lane < 24, low, 0.0))).astype(BF16)
    same = lax.broadcasted_iota(jnp.int32, (32, 128), 0) == lax.broadcasted_iota(jnp.int32, (32, 128), 1)
    pick = jnp.where(same, 1.0, 0.0).astype(BF16)
    for at, (ref, index) in enumerate(places):
        pack_levels(ref, index, mm_t(pick, packed[at * ROWS : (at + 1) * ROWS]))


def attend(query, keys, values, first, count, together):
    shape = (RING, TALL, HALF) if together else (1, TALL, HALF)
    spans = RING // count if together else 1
    outs = 1 if together else count
    block = (count if together else 1, TALL, HALF)
    return pl.pallas_call(
        attend_kernel,
        grid=(spans,),
        in_specs=[
            pl.BlockSpec((pl.Element(count), pl.Element(ROWS), pl.Element(HALF)), lambda i: (first + i * count, 0, 0)),
            VMEM,
            VMEM,
        ],
        out_specs=[pl.BlockSpec(block, lambda i: (i, 0, 0))] * outs,
        out_shape=[jax.ShapeDtypeStruct(shape, BF16)] * outs,
        compiler_params=pltpu.CompilerParams(vmem_limit_bytes=VMEM_LIMIT),
        name="attend",
    )(query, keys, values)


def join_parts(parts):
    row = lax.broadcasted_iota(jnp.int32, (32, HALF), 0)
    column = lax.broadcasted_iota(jnp.int32, (32, HALF), 1)
    spread = jnp.where(((row & 7) == (column >> 6)) & (row < 24), 1.0, 0.0).astype(BF16)
    levels = []
    for ref, index in parts:
        compact = jnp.concatenate(
            [ref[index, ROWS:TALL, 0:ROWS], ref[index, ROWS:TALL, 256 : 256 + ROWS]], axis=0
        )
        levels.append(
            lax.dot_general(compact, spread, (((0,), (0,)), ((), ())), preferred_element_type=F32)
        )
    top = levels[0]
    for level in levels[1:]:
        top = jnp.maximum(top, level)
    total = None
    mixed = None
    for (ref, index), level in zip(parts, levels):
        weight = jnp.exp2(level - top)
        value = weight * ref[index, 0:ROWS, :].astype(F32)
        total = weight if total is None else total + weight
        mixed = value if mixed is None else mixed + value
    return mixed / total, top, total


def join_kernel(parts_ref, out_ref):
    result, top, total = join_parts([(parts_ref, at) for at in range(RING)])
    out_ref[0, 0:ROWS, :] = result.astype(BF16)
    row = lax.broadcasted_iota(jnp.int32, (8, HALF), 0)
    column = lax.broadcasted_iota(jnp.int32, (8, HALF), 1)
    pick = jnp.where(row * HEAD_DIM == column, 1.0, 0.0).astype(BF16)
    pieces = [mm_t(pick, piece.astype(BF16)) for piece in split3(top + jnp.log2(total))]
    pack_levels(out_ref, 0, jnp.concatenate(pieces + [jnp.zeros((8, ROWS), F32)], axis=0))


def join(parts):
    return pl.pallas_call(
        join_kernel,
        out_shape=jax.ShapeDtypeStruct((1, TALL, HALF), BF16),
        compiler_params=pltpu.CompilerParams(vmem_limit_bytes=8 * MIB),
        name="join",
    )(parts)


def merge_kernel(out_ref, *refs):
    parts, (mine_ref, send_ref) = refs[:-2], refs[-2:]
    core = lax.axis_index("h")
    result, _, _ = join_parts([(ref, 0) for ref in parts])
    attended = result.astype(BF16)
    mine_ref[...] = mm(attended, out_ref[:, pl.ds(pl.multiple_of(core * HALF, HALF), HALF)])
    send_ref[...] = mm(attended, out_ref[:, pl.ds(pl.multiple_of((1 - core) * HALF, HALF), HALF)]).astype(BF16)


def merge(render_out, parts):
    return pl.pallas_call(
        merge_kernel,
        in_specs=[VMEM] * (1 + len(parts)),
        out_specs=[VMEM] * 2,
        out_shape=[
            jax.ShapeDtypeStruct((ROWS, HALF), F32),
            jax.ShapeDtypeStruct((ROWS, HALF), BF16),
        ],
        compiler_params=pltpu.CompilerParams(vmem_limit_bytes=10 * MIB),
        name="merge",
    )(render_out, *parts)


def shift(value, axis, size, by):
    return lax.ppermute(value, axis, [(at, (at + by) % size) for at in range(size)])


def local(
    tokens,
    frame_order,
    target_mask,
    pose_norm,
    pose_qkv,
    pose_out,
    camera_head,
    ray_embed,
    render_norm,
    render_qkv,
    render_out,
):
    send, near, far = start(frame_order, target_mask, tokens)

    def other(value):
        return shift(value, "h", 2, 1)

    def step_up(value):
        return shift(value, "z", 8, 1)

    def step_down(value):
        return shift(value, "z", 8, 7)

    tie = lax.optimization_barrier
    cam_all = lax.all_to_all(send, ("x", "y", "z"), 0, 0)
    up1, down1, across = step_up(near), step_down(near), shift(near, "y", 2, 1)
    opposite = shift(near, "z", 8, 4)
    planes = jnp.stack([near, across])
    cam_all, up1, down1, planes = tie((cam_all, up1, down1, planes))
    up2, down2 = step_up(up1), step_down(down1)
    side1, side3, side2 = (shift(planes, "x", 4, by) for by in (1, 3, 2))
    cams = pose(cam_all, pose_norm[None, :], pose_qkv, pose_out, camera_head.T)
    cams, up2, down2, opposite = tie((cams, up2, down2, opposite))
    more = other(cams)
    up3, down3 = step_up(up2), step_down(down2)
    more, up3, down3, side1, side3, side2 = tie((more, up3, down3, side1, side3, side2))
    gain = render_norm.reshape(2, 1, HALF)
    qkv = render_qkv.reshape(3, 2, HALF, HALF)

    def pair(value):
        return (value, other(value))

    own_pair = (near, far)
    key, val, query, share, own = prep(
        ((0, 1), (7, 2, 6), (4, 3, 5)),
        (((0, 0), (0, 1)), ((1, 0), (1, 1), (3, 0), (3, 1)), ((2, 0), (2, 1))),
        cams,
        more,
        ray_embed,
        gain,
        qkv,
        [own_pair]
        + [pair(value) for value in (up1, down1, up2, down2, opposite, up3, down3)]
        + [own_pair]
        + [pair(value) for value in (across, side1, side3, side2)],
    )
    far_parts = lax.all_to_all(attend(query, key, val, RING, 2, True)[0], "x", 0, 0)
    sides = [shift(part, "x", 4, -by) for by, part in zip((1, 2, 3), attend(query, key, val, 1, 3, False))]
    crossed = join(far_parts)
    query, crossed = tie((query, crossed))
    crossed = shift(crossed, "y", 2, 1)
    nearest = attend(query, key, val, 0, 1, False)
    mine, outgoing = merge(render_out, [*nearest, crossed, *sides])
    theirs = other(outgoing)
    rendered = (share.astype(F32) + (mine + theirs.astype(F32))).astype(BF16)
    return (rendered, own)


def solution(mesh):
    fine = Mesh(mesh.devices.reshape(4, 2, 8, 2, 2), ("x", "y", "z", "h", "dp"))
    rows = ("dp", "x", "y", "z")
    in_specs = (
        P(rows, None),
        P(rows),
        P(rows),
        P(),
        P(None, None, "h"),
        P("h", None),
        P(),
        P(),
        P(),
        P(None, None, "h"),
        P("h", None),
    )
    out_specs = (P(rows, "h"), P(rows, None))
    return jax.shard_map(local, mesh=fine, in_specs=in_specs, out_specs=out_specs, check_vma=False)
```
